512 devices in a mesh: section: 8 (over y, core), shard: 64 (over x, z).
Axes of the slice: x: 4, y: 4, z: 16, core: 2. Of those that a mesh axis runs over, the one named last changes fastest.
Arguments:
- top_grad: bfloat16 [2, 8192, 1024], P(None, 'shard'), may hold values from -6 to 6
- layer_inputs: bfloat16 [8, 2, 8192, 1024], P('section', None, 'shard'), may hold values from -6 to 6
- saved_pre: bfloat16 [8, 2, 8192, 2048], P('section', None, 'shard'), may hold values from -6 to 6
- weight_in: bfloat16 [8, 1024, 2048], P('section', 'shard'), may hold values from -0.1875 to 0.1875
- weight_out: bfloat16 [8, 512, 1024], P('section', 'shard'), may hold values from -0.25 to 0.25
- gain_in: float32 [8, 1024], P('section'), may hold values from 0.1 to 1.9
- gain_mid: float32 [8, 512], P('section'), may hold values from 0.1 to 1.9
- lengths: int32 [2, 64, 4], P(None, 'shard'), may hold values from 1 to 64, 128 in all within a row
- quot_ids: int32 [2, 8192], P(None, 'shard'), may hold values from 0 to 4095, as said below
- rem_ids: int32 [2, 8192], P(None, 'shard'), may hold values from 0 to 4095, as said below
Outputs:
- quot_grad: float32 [4096, 1024], P('shard', 'section')
- rem_grad: float32 [4096, 1024], P('shard', 'section')
The draws below stay inside these ranges and needn't reach their ends.
Inputs may be any that keep to these rules, and one draw needn't show every extreme that they name: `quot_ids`: table rows are owned in blocks of 64 consecutive ids, block o by shard index o. The 2 micro-batches' tokens of one shard index name ids of any one block at most 8 times; in every draw two blocks are named exactly 8 times by the tokens of every shard index. `rem_ids`: as for quot_ids.
All inputs are finite; a program needn't handle non-finite values.
Results may differ from the reference program's by a relative error of at most 0.034.
Values may be sent and summed in bfloat16 or wider, within the bound.
No kernel may reach another device: no remote copies, remote signals or barrier semaphores. Data moves between devices by JAX's collectives and lax.ppermute only.
A program may use at most 64 MiB of HBM per device.

```python
import math
import jax
import jax.numpy as jnp
import numpy as np
from jax import lax

D = 1024
HEADS = 4
ATT = 512
LAYERS = 8
MICRO = 2
TOK_DEV = 128
TOKENS = 8192
SEQS = 4
L_MAX = 64
QROW_DEV = 64
TABLE_ROWS = 4096
N_SHARD = 64


def table_ids(key):
    block_len = MICRO * TOK_DEV
    capacity = max(2, 2 * (block_len // N_SHARD))
    shard_count = TOKENS // TOK_DEV
    shared_key, device_key = jax.random.split(key)
    shared = jax.random.permutation(shared_key, N_SHARD)

    def one_device(own_key):
        order_key, spare_key, row_key = jax.random.split(own_key, 3)
        grouped = jax.random.permutation(order_key, block_len) // capacity
        spare = jax.random.permutation(spare_key, N_SHARD - 2)
        picked = jnp.where(grouped < 2, grouped, 2 + spare[jnp.clip(grouped - 2, 0, N_SHARD - 3)])
        owners = shared[picked]
        offsets = jax.random.randint(row_key, (block_len,), 0, QROW_DEV)
        return (owners * QROW_DEV + offsets).astype(jnp.int32)
    per_device = jax.vmap(one_device)(jax.random.split(device_key, shard_count))
    return per_device.reshape(shard_count, MICRO, TOK_DEV).transpose(1, 0, 2).reshape(MICRO, TOKENS)


def draw_quot_ids(key, part):
    key = jax.random.fold_in(key, 7)
    return table_ids(key)


def draw_rem_ids(key, part):
    key = jax.random.fold_in(key, 8)
    return table_ids(key)


def steps_of(rng, dims, pieces, least, high):
    factor_of = 1.0
    for dim, shards_of in pieces:
        heights = jax.random.uniform(jax.random.fold_in(jax.random.fold_in(rng, 6), dim), (shards_of,), jnp.float32, least / len(pieces), high / len(pieces))
        factor_of = factor_of * jnp.repeat(jnp.exp(heights), dims[dim] // shards_of).reshape((-1,) + (1,) * (len(dims) - 1 - dim))
    return factor_of


def profile(number_of, total, most, slope):
    loads = [(1 << 20) // math.isqrt(standing ** slope) + 1 for standing in range(2, number_of + 1)]
    surplus, counts = total - most - (number_of - 1), [1] * (number_of - 1)
    while surplus > 0:
        movable = [i for i in range(number_of - 1) if counts[i] < most]
        pool, remaining = sum([loads[i] for i in movable]), surplus
        for i in movable:
            extra = min(most - counts[i], max(1, remaining * loads[i] // pool), surplus)
            counts[i] = counts[i] + extra
            surplus = surplus - extra
    return np.array([most] + counts)


def uneven(stream_key, amount, total, limit, skew):
    if amount == 2:
        one = jax.random.randint(stream_key, (), max(1, total - limit), min(limit, total - 1) + 1)
        return jnp.stack([one, total - one])
    sizes = jnp.asarray(profile(amount, total, limit, skew), jnp.int32)
    twos = (amount - 1) // 2
    giver, receiver = sizes[1:1 + 2 * twos:2], sizes[2:2 + 2 * twos:2]
    room = jnp.minimum(giver - 1, limit - receiver)
    passed = jax.random.randint(jax.random.fold_in(stream_key, 1), (twos,), 0, 1 << 20) % (room + 1)
    sizes = sizes.at[1:1 + 2 * twos:2].set(giver - passed).at[2:2 + 2 * twos:2].set(receiver + passed)
    return sizes[jax.random.permutation(jax.random.fold_in(stream_key, 2), amount)]


def bell_draw(key, shape, deviation, reach, cuts=(), kind=jnp.bfloat16):
    entries = jax.random.normal(key, shape, jnp.float32) * deviation
    if len(cuts) > 0:
        entries = steps_of(key, shape, cuts, -0.22, 0.18) * entries
    return jnp.clip(entries, min=-reach, max=reach).astype(kind)


def setup_inputs(seed: int = 0) -> dict:
    arg_keys = jax.random.split(jax.random.key(seed), 11)
    return {
        "top_grad": bell_draw(arg_keys[0], (MICRO, TOKENS, D), 1.0, 6.0, ((1, 64),)),
        "layer_inputs": bell_draw(arg_keys[1], (LAYERS, MICRO, TOKENS, D), 1.0, 6.0, ((0, 8), (2, 64))),
        "saved_pre": bell_draw(arg_keys[2], (LAYERS, MICRO, TOKENS, 4 * ATT), 1.0, 6.0, ((0, 8), (2, 64))),
        "weight_in": bell_draw(arg_keys[3], (LAYERS, D, 4 * ATT), D ** -0.5, 0.1875, ((0, 8), (1, 64))),
        "weight_out": bell_draw(arg_keys[4], (LAYERS, ATT, D), ATT ** -0.5, 0.25, ((0, 8), (1, 64))),
        "gain_in": jnp.clip(1.0 + 0.18 * jax.random.normal(arg_keys[5], (LAYERS, D), jnp.float32), 0.1, 1.9),
        "gain_mid": jnp.clip(1.0 + 0.18 * jax.random.normal(arg_keys[6], (LAYERS, ATT), jnp.float32), 0.1, 1.9),
        "lengths": jax.vmap(lambda own: uneven(own, SEQS, TOK_DEV, L_MAX, 2))(jax.random.split(arg_keys[7], MICRO * N_SHARD)).reshape((MICRO, N_SHARD, SEQS)).astype(jnp.int32),
        "quot_ids": draw_quot_ids(jax.random.fold_in(arg_keys[10], 71), 0),
        "rem_ids": draw_rem_ids(jax.random.fold_in(arg_keys[10], 71), 0),
    }


EPSILON = 1e-05

def layer_norm(operand, gain_vec):
    average = lax.optimization_barrier(jnp.mean(operand, axis=-1, keepdims=True))
    centred = operand - average
    spread = lax.optimization_barrier(jnp.mean(centred * centred, axis=-1, keepdims=True))
    return centred * lax.rsqrt(spread + EPSILON) * gain_vec

def segments_of(seq_len, row_count):
    seq_ends = jnp.cumsum(seq_len)
    places = jnp.arange(row_count, dtype=jnp.int32)
    return lax.optimization_barrier(jnp.sum((places[:, None] >= seq_ends[None, :]).astype(jnp.int32), axis=1))

def mixing(pre_values, segment, gain_mid):
    row_count = pre_values.shape[0]
    inner_width = pre_values.shape[1] // 4
    head_size = inner_width // HEADS
    activated = jax.nn.silu(pre_values)
    gating, values, queries, key_rows = jnp.split(activated, 4, axis=1)
    queries = queries.reshape(row_count, HEADS, head_size)
    key_rows = key_rows.reshape(row_count, HEADS, head_size)
    values = values.reshape(row_count, HEADS, head_size)
    scores = jnp.einsum('ihd,jhd->hij', queries, key_rows, precision=lax.Precision.HIGHEST) / math.sqrt(head_size)
    places = jnp.arange(row_count, dtype=jnp.int32)
    allowed = (segment[:, None] == segment[None, :]) & (places[None, :] <= places[:, None])
    weights = jnp.where(allowed[None, :, :], jax.nn.silu(scores), jnp.zeros_like(scores))
    mixture = jnp.einsum('hij,jhd->ihd', weights, values, precision=lax.Precision.HIGHEST).reshape(row_count, inner_width)
    return layer_norm(mixture, gain_mid) * gating

def layer_back(grad_out, inputs, pre_values, weight_in, weight_out, gain_in, gain_mid, segment):
    grad_mid = lax.dot_general(grad_out, weight_out, (((1,), (1,)), ((), ())), preferred_element_type=jnp.float32)
    pullback = jax.vjp(lambda operand: mixing(operand, segment, gain_mid), pre_values.astype(jnp.float32))[1]
    grad_pre = pullback(grad_mid)[0].astype(jnp.bfloat16)
    grad_norm = lax.dot_general(grad_pre, weight_in, (((1,), (1,)), ((), ())), preferred_element_type=jnp.float32)
    pull_input = jax.vjp(lambda operand: layer_norm(operand, gain_in), inputs.astype(jnp.float32))[1]
    return (grad_out.astype(jnp.float32) + pull_input(grad_norm)[0]).astype(jnp.bfloat16)

def reference(top_grad, layer_inputs, saved_pre, weight_in, weight_out, gain_in, gain_mid, lengths, quot_ids, rem_ids):
    shard_count = lengths.shape[1]
    segment = jax.vmap(jax.vmap(lambda seq_len: segments_of(seq_len, TOK_DEV)))(lengths)
    inner = jax.vmap(layer_back, in_axes=(0, 0, 0, None, None, None, None, 0))
    backward = jax.vmap(inner, in_axes=(0, 0, 0, None, None, None, None, 0))

    def blocks(tensor):
        return tensor.reshape(MICRO, shard_count, TOK_DEV, tensor.shape[-1])
    carried = blocks(top_grad)
    for layer_idx in reversed(range(LAYERS)):
        carried = backward(carried, blocks(layer_inputs[layer_idx]), blocks(saved_pre[layer_idx]), weight_in[layer_idx], weight_out[layer_idx], gain_in[layer_idx], gain_mid[layer_idx], segment)
    flat_grads = carried.reshape(MICRO * shard_count * TOK_DEV, D).astype(jnp.float32)
    quot_grad = jax.ops.segment_sum(flat_grads, quot_ids.reshape(-1), num_segments=TABLE_ROWS)
    rem_grad = jax.ops.segment_sum(flat_grads, rem_ids.reshape(-1), num_segments=TABLE_ROWS)
    return (quot_grad, rem_grad)
```

```python
import functools
import math

import jax
import jax.numpy as jnp
from jax import lax
from jax.experimental import pallas as pl
from jax.experimental.pallas import tpu as pltpu
from jax.sharding import PartitionSpec as P

HEADS = 4
HEAD = 128
ATT = 512
ROWS = 128
WIDTH = 1024
SECTIONS = 8
MICRO = 2
SHARDS = 64
X_SIZE = 4
Z_SIZE = 16
QROW_DEV = 64
CAP = 8
SLOTS = SHARDS * 2 * CAP
EPSILON = 1e-05
BF16 = jnp.bfloat16
F32 = jnp.float32
MIB = 1024 * 1024
VMEM = pl.BlockSpec(memory_space=pltpu.VMEM)
HBM = pl.BlockSpec(memory_space=pl.ANY)

UGR, XHAT, EU, SV, SQ, SK, KT, QT, VN, AN, PT = range(11)
SAVED = 11


def nt(a, b):
    return lax.dot_general(a, b, (((1,), (1,)), ((), ())), preferred_element_type=F32)


def nn(a, b):
    return jnp.dot(a, b, preferred_element_type=F32)


def params(mib):
    return pltpu.CompilerParams(vmem_limit_bytes=mib * MIB)


def cost(flops, size):
    return pl.CostEstimate(flops=flops, bytes_accessed=size, transcendentals=0)


def segment_grid(len_ref, micro, dim):
    place = lax.broadcasted_iota(jnp.int32, (ROWS, ROWS), dim)
    end = jnp.int32(0)
    seg = jnp.zeros((ROWS, ROWS), jnp.int32)
    for k in range(4):
        end = end + len_ref[micro, k]
        seg = seg + (place >= end).astype(jnp.int32)
    return place, seg


def forward_kernel(len_ref, pre_hbm, x_hbm, top_hbm, gain_mid_ref, gain_in_ref, gain_t_ref, *refs):
    out_refs, (pre_ref, x_ref, top_ref, sems) = refs[:4 * MICRO], refs[4 * MICRO:]
    copies = []
    for k, (src, dst) in enumerate(((pre_hbm, pre_ref), (x_hbm, x_ref), (top_hbm, top_ref))):
        for micro in range(MICRO):
            copies.append(pltpu.make_async_copy(src.at[micro], dst.at[micro], sems.at[k, micro]))
            copies[-1].start()
    gain_t_ref[...] = jnp.broadcast_to(gain_in_ref[...], (ROWS, WIDTH)).T
    for one in copies:
        one.wait()
    for micro in range(MICRO):
        saved_ref, xh_ref, rstd_ref, top_t_ref = out_refs[4 * micro:4 * micro + 4]
        forward_part(len_ref, micro, pre_ref, x_ref, top_ref, gain_mid_ref[...],
                     saved_ref, xh_ref, rstd_ref, top_t_ref)


def forward_part(len_ref, micro, pre_ref, x_ref, top_ref, gain, saved_ref, xh_ref, rstd_ref, top_t_ref):
    def act(block):
        pre = pre_ref[micro, :, block * ATT:(block + 1) * ATT].astype(F32)
        sig = jax.nn.sigmoid(pre)
        return pre * sig, sig * (1.0 + pre * (1.0 - sig))

    row, seg_row = segment_grid(len_ref, micro, 0)
    col, seg_col = segment_grid(len_ref, micro, 1)
    same = seg_row == seg_col
    allowed = same & (col <= row)
    allowed_t = same & (row <= col)
    val, dval = act(1)
    que, dque = act(2)
    key, dkey = act(3)
    saved_ref[SV] = dval.T.astype(BF16)
    saved_ref[SQ] = dque.T.astype(BF16)
    saved_ref[SK] = dkey.T.astype(BF16)
    saved_ref[KT] = key.T.astype(BF16)
    saved_ref[QT] = que.T.astype(BF16)
    val, que, key = val.astype(BF16), que.astype(BF16), key.astype(BF16)
    scale = 1.0 / math.sqrt(HEAD)
    mixture = []
    for h in range(HEADS):
        cols = slice(h * HEAD, (h + 1) * HEAD)
        scores = nt(que[:, cols], key[:, cols]) * scale
        soft = jnp.where(allowed, scores * jax.nn.sigmoid(scores), 0.0).astype(BF16)
        scores = nt(key[:, cols], que[:, cols]) * scale
        sig = jax.nn.sigmoid(scores)
        slope = jnp.where(allowed_t, sig * (1.0 + scores * (1.0 - sig)) * scale, 0.0)
        saved_ref[VN, cols, :] = val[:, cols]
        saved_ref[AN, cols, :] = soft
        saved_ref[PT, cols, :] = slope.astype(BF16)
        mixture.append(nn(soft, val[:, cols]))
    mixture = jnp.concatenate(mixture, axis=1)
    centred = mixture - jnp.mean(mixture, axis=1, keepdims=True)
    rstd = lax.rsqrt(jnp.mean(centred * centred, axis=1, keepdims=True) + EPSILON)
    xhat = centred * rstd
    gate, dgate = act(0)
    saved_ref[UGR] = (gate * gain * rstd).T.astype(BF16)
    saved_ref[XHAT] = xhat.T.astype(BF16)
    saved_ref[EU] = (xhat * gain * dgate).T.astype(BF16)
    x = x_ref[micro].astype(F32).T
    x = x - jnp.mean(x, axis=0, keepdims=True)
    rstd = lax.rsqrt(jnp.mean(x * x, axis=0, keepdims=True) + EPSILON)
    xh_ref[...] = (x * rstd).astype(BF16)
    rstd_ref[...] = jnp.broadcast_to(rstd, (8, ROWS))
    top_t_ref[...] = top_ref[micro].astype(F32).T.astype(BF16)


def forward(lengths, pre, x, top, gain_mid, gain_in):
    smem = pl.BlockSpec(memory_space=pltpu.SMEM)
    tall = jax.ShapeDtypeStruct((WIDTH, ROWS), BF16)
    each = [
        jax.ShapeDtypeStruct((SAVED, ATT, ROWS), BF16),
        tall,
        jax.ShapeDtypeStruct((8, ROWS), F32),
        tall,
    ]
    return pl.pallas_call(
        forward_kernel,
        in_specs=[smem] + [pl.BlockSpec(memory_space=pltpu.HBM)] * 3 + [VMEM] * 2,
        out_specs=[VMEM] * 9,
        out_shape=[jax.ShapeDtypeStruct((WIDTH, ROWS), F32)] + each * MICRO,
        scratch_shapes=[
            pltpu.VMEM((MICRO, ROWS, 4 * ATT), BF16),
            pltpu.VMEM((MICRO, ROWS, WIDTH), BF16),
            pltpu.VMEM((MICRO, ROWS, WIDTH), BF16),
            pltpu.SemaphoreType.DMA((3, MICRO)),
        ],
        compiler_params=params(32),
        cost_estimate=cost(2 * 10**8, 6 * MIB),
        name="saved_parts",
    )(lengths, pre, x, top, gain_mid, gain_in)


HALVES = 2048
IDS = HALVES + 512
LINE = IDS + ROWS


def join_kernel(w_in_hbm, w_out_hbm, quot_hbm, rem_hbm, out_ref, w_in, w_out, quot, rem, sems):
    copies = []
    for k, pair in enumerate(((w_in_hbm, w_in), (w_out_hbm, w_out), (quot_hbm, quot), (rem_hbm, rem))):
        copies.append(pltpu.make_async_copy(*pair, sems.at[k]))
        copies[-1].start()
    for one in copies:
        one.wait()
    out_ref[:, :HALVES] = w_in[0]
    wide = w_out[0].astype(F32)
    halves = jnp.concatenate([wide[:, :512], wide[:, 512:]], axis=0)
    out_ref[:, HALVES:IDS] = halves.astype(BF16)
    ids = jnp.concatenate([quot[...], rem[...]], axis=0)
    owner = lax.shift_right_logical(ids, 6)
    local = ids - owner * QROW_DEV
    blank = jnp.zeros((8, ROWS), F32)
    coded = jnp.concatenate([owner.astype(F32), local.astype(F32), blank], axis=0)
    out_ref[:, IDS:] = coded.astype(BF16)


def pair_kernel(own_ref, next_ref, out_ref):
    out_ref[0:16, :] = own_ref[...]
    out_ref[16:32, :] = next_ref[...]


def pick_kernel(which, n_blocks, gated, n_after, *refs):
    outs = refs[n_blocks + gated + n_after:]
    if gated:
        outs[1][...] = refs[n_blocks][...]
    for k, ref in enumerate(refs[:n_blocks]):
        outs[0][k * 16:(k + 1) * 16, :] = ref[which * 16:(which + 1) * 16, :]


def pick(which, blocks, gate=None, after=()):
    gates = [] if gate is None else [gate]
    shapes = [jax.ShapeDtypeStruct((16 * len(blocks), LINE), BF16)]
    shapes += [jax.ShapeDtypeStruct((32, LINE), BF16)] * len(gates)
    return pl.pallas_call(
        functools.partial(pick_kernel, which, len(blocks), len(gates), len(after)),
        in_specs=[VMEM] * (len(blocks) + len(gates)) + [HBM] * len(after),
        out_specs=[VMEM] * len(shapes),
        out_shape=shapes,
        compiler_params=params(16),
        cost_estimate=cost(1000, len(blocks) * 160 * 1024),
        name="pick_shards",
    )(*blocks, *gates, *after)


def along(value, dx, dz):
    pairs = []
    for x in range(X_SIZE):
        for z in range(Z_SIZE):
            to = (x + dx) % X_SIZE * Z_SIZE + (z + dz) % Z_SIZE
            pairs.append((x * Z_SIZE + z, to))
    return lax.ppermute(value, "shard", pairs)


def gather_weights(weight_in, weight_out, quot_ids, rem_ids):
    own = pl.pallas_call(
        join_kernel,
        in_specs=[pl.BlockSpec(memory_space=pltpu.HBM)] * 4,
        out_specs=VMEM,
        out_shape=jax.ShapeDtypeStruct((16, LINE), BF16),
        scratch_shapes=[
            pltpu.VMEM((1, 16, 2048), BF16),
            pltpu.VMEM((1, 8, 1024), BF16),
            pltpu.VMEM((MICRO, ROWS), jnp.int32),
            pltpu.VMEM((MICRO, ROWS), jnp.int32),
            pltpu.SemaphoreType.DMA((4,)),
        ],
        compiler_params=params(56),
        cost_estimate=cost(1000, 160 * 1024),
        name="join_weights",
    )(weight_in, weight_out, quot_ids, rem_ids)
    block = pl.pallas_call(
        pair_kernel,
        in_specs=[VMEM, VMEM],
        out_specs=VMEM,
        out_shape=jax.ShapeDtypeStruct((32, LINE), BF16),
        compiler_params=params(16),
        cost_estimate=cost(1000, 320 * 1024),
        name="pair_weights",
    )(own, along(own, -1, 0))
    up, down = {0: block}, {}
    half = Z_SIZE // 2
    blocks, offsets, below, above = [], [], [], []

    def batch_of(hops):
        batch = []
        for hop in hops:
            batch.append(up[hop])
            offsets.append(-hop)
            if hop in down:
                batch.append(down[hop])
                offsets.append(hop)
        blocks.extend(batch)
        return batch

    gates = {3: (0, 1), 5: (2, 3), 7: (4, 5), 8: (6,)}
    for hop in range(1, half + 1):
        if hop in gates:
            batch = batch_of(gates[hop])
            picked, up[hop - 1] = pick(0, batch, up[hop - 1], below[-1:])
            below.append(along(picked, 1, 0))
        up[hop] = along(up[hop - 1], 0, 1)
        last = down[hop - 1] if hop > 1 else block
        if hop in gates:
            if hop < half:
                picked, last = pick(1, batch, last, above[-1:])
                down[hop - 1] = last
            else:
                picked = pick(1, batch, None, above[-1:])[0]
            above.append(along(picked, -1, 0))
        if hop < half:
            down[hop] = along(last, 0, -1)
    for hops in ((half - 1,), (half,)):
        batch = batch_of(hops)
        below.append(along(pick(0, batch)[0], 1, 0))
        above.append(along(pick(1, batch)[0], -1, 0))
    sizes = [x.shape[0] // 16 for x in below]
    return pl.pallas_call(
        functools.partial(place_kernel, tuple(offsets), tuple(sizes)),
        in_specs=[VMEM] * (Z_SIZE + 2 * len(sizes)),
        out_specs=[VMEM] * 3,
        out_shape=[
            jax.ShapeDtypeStruct((Z_SIZE, 64, 2048), BF16),
            jax.ShapeDtypeStruct((Z_SIZE, 32, 1024), BF16),
            jax.ShapeDtypeStruct((Z_SIZE, X_SIZE, 16, ROWS), BF16),
        ],
        scratch_shapes=[pltpu.VMEM((Z_SIZE, 32, 1024), F32)],
        compiler_params=params(32),
        cost_estimate=cost(1000, 10 * MIB),
        name="place_weights",
    )(*blocks, *below, *above)


def place_kernel(offsets, sizes, *refs):
    blocks, refs = refs[:Z_SIZE], refs[Z_SIZE:]
    below, above = refs[:len(sizes)], refs[len(sizes):2 * len(sizes)]
    w_in_ref, w_out_ref, ids_ref, wide = refs[2 * len(sizes):]
    here_x = lax.axis_index("shard") // Z_SIZE
    here_z = lax.axis_index("shard") % Z_SIZE
    spots = [(batch, k) for batch, size in enumerate(sizes) for k in range(size)]
    for block, offset, (batch, k) in zip(blocks, offsets, spots):
        z = (here_z + Z_SIZE + offset) % Z_SIZE
        rows = slice(k * 16, (k + 1) * 16)
        shards_of = ((block, slice(0, 16)), (block, slice(16, 32)), (above[batch], rows), (below[batch], rows))
        for step, (ref, rows) in enumerate(shards_of):
            x = (here_x + step) % X_SIZE
            w_in_ref[z, pl.ds(pl.multiple_of(x * 16, 16), 16), :] = ref[rows, :HALVES]
            ids_ref[z, x] = ref[rows, IDS:]
            halves = ref[rows, HALVES:IDS].astype(F32)
            at = pl.ds(pl.multiple_of(x * 8, 8), 8)
            wide[z, at, 0:512] = halves[0:8]
            wide[z, at, 512:1024] = halves[8:16]
    for z in range(Z_SIZE):
        w_out_ref[z] = wide[z].astype(BF16)


def step_kernel(at_section, last, n_extra, *refs):
    refs = list(refs)
    g_ref = refs.pop(0)
    first_ref = refs.pop(0) if last else None
    saved, xh, rstd, gain, w_in, w_out = refs[:6]
    outs, gp = refs[6 + n_extra:-1], refs[-1]

    @pl.when(lax.axis_index("section") == at_section)
    def _():
        grad = g_ref[...]
        product = nn(w_out[...].reshape(ATT, WIDTH), grad).reshape(Z_SIZE, HEADS, 8, ROWS)
        grad_mid = [product[:, h].reshape(HEAD, ROWS) for h in range(HEADS)]

        def part(name, h):
            return saved[name, h * HEAD:(h + 1) * HEAD, :]

        terms = [grad_mid[h] * part(UGR, h).astype(F32) for h in range(HEADS)]
        xhats = [part(XHAT, h).astype(F32) for h in range(HEADS)]
        mean_1 = sum(terms[1:], terms[0])
        mean_2 = terms[0] * xhats[0]
        for h in range(1, HEADS):
            mean_2 = mean_2 + terms[h] * xhats[h]
        mean_1 = jnp.sum(mean_1, axis=0, keepdims=True) * (1.0 / ATT)
        mean_2 = jnp.sum(mean_2, axis=0, keepdims=True) * (1.0 / ATT)
        for h in range(HEADS):
            def put(block, value):
                start = block * ATT + h * HEAD
                gp[start:start + HEAD, :] = value.astype(BF16)

            put(0, grad_mid[h] * part(EU, h).astype(F32))
            d_o = (terms[h] - mean_1 - xhats[h] * mean_2).astype(BF16)
            d_s = (nn(part(VN, h), d_o) * part(PT, h).astype(F32)).astype(BF16)
            put(1, nn(d_o, part(AN, h)) * part(SV, h).astype(F32))
            put(2, nn(part(KT, h), d_s) * part(SQ, h).astype(F32))
            put(3, nt(part(QT, h), d_s) * part(SK, h).astype(F32))
        product = nn(w_in[...].reshape(WIDTH, 4 * ATT), gp[...])
        product = product.reshape(Z_SIZE, X_SIZE, 16, ROWS)
        d_xh, x_hat = [], []
        for x in range(X_SIZE):
            rows = slice(x * 256, (x + 1) * 256)
            d_xh.append(product[:, x].reshape(256, ROWS) * gain[rows, :])
            x_hat.append(xh[rows, :].astype(F32))
        mean_1 = sum(d_xh[1:], d_xh[0])
        mean_2 = d_xh[0] * x_hat[0]
        for x in range(1, X_SIZE):
            mean_2 = mean_2 + d_xh[x] * x_hat[x]
        mean_1 = jnp.sum(mean_1, axis=0, keepdims=True) * (1.0 / WIDTH)
        mean_2 = jnp.sum(mean_2, axis=0, keepdims=True) * (1.0 / WIDTH)
        scale = rstd[0:1, :]
        for x in range(X_SIZE):
            rows = slice(x * 256, (x + 1) * 256)
            d_x = (d_xh[x] - mean_1 - x_hat[x] * mean_2) * scale
            result = (grad[rows, :].astype(F32) + d_x).astype(BF16)
            if last:
                outs[x][ROWS:2 * ROWS, :] = result[0:128]
                outs[x][3 * ROWS:, :] = result[128:256]
            else:
                outs[0][rows, :] = result
        if last:
            for x in range(X_SIZE):
                outs[x][0:ROWS, :] = first_ref[x * 256:x * 256 + 128, :]
                outs[x][2 * ROWS:3 * ROWS, :] = first_ref[x * 256 + 128:(x + 1) * 256, :]


def layer_step(at_section, grad, first, kept, weights, extra):
    last = first is not None
    operands = [grad, first] if last else [grad]
    operands += [*kept, *weights]
    if last:
        out_shape = [jax.ShapeDtypeStruct((4 * ROWS, ROWS), BF16)] * (SECTIONS // 2)
    else:
        out_shape = [jax.ShapeDtypeStruct((WIDTH, ROWS), BF16)]
    out = pl.pallas_call(
        functools.partial(step_kernel, at_section, last, len(extra)),
        in_specs=[VMEM] * len(operands) + [HBM] * len(extra),
        out_specs=[VMEM] * len(out_shape),
        out_shape=out_shape,
        scratch_shapes=[pltpu.VMEM((4 * ATT, ROWS), BF16)],
        compiler_params=params(32),
        cost_estimate=cost(7 * 10**8, 8 * MIB),
        name="layer_step",
    )(*operands, *extra)
    return out if last else out[0]


def earlier_mask():
    tokens = MICRO * ROWS
    before = (
        lax.broadcasted_iota(jnp.int32, (tokens, tokens), 0)
        < lax.broadcasted_iota(jnp.int32, (tokens, tokens), 1)
    )
    return jnp.where(before, 1.0, 0.0).astype(BF16)


def slots_kernel(quot_ref, rem_ref, _, slot_ref):
    owners = lax.broadcasted_iota(jnp.int32, (SHARDS, MICRO * ROWS), 0)
    before = earlier_mask()
    for table, ref in enumerate((quot_ref, rem_ref)):
        ids = jnp.concatenate([ref[0:1, :], ref[1:2, :]], axis=1)
        owner = lax.shift_right_logical(ids, 6)
        one_hot = jnp.where(owners == owner, 1.0, 0.0)
        earlier = nn(one_hot.astype(BF16), before)
        rank = jnp.sum(earlier * one_hot, axis=0, keepdims=True).astype(jnp.int32)
        slot_ref[table:table + 1, :] = owner * (2 * CAP) + rank + table * CAP


def rows_kernel(ids_ref, _, rows_ref, wide_ids):
    here = lax.axis_index("shard").astype(F32)
    before = earlier_mask()
    lane = lax.broadcasted_iota(jnp.int32, (SHARDS, 128), 1)
    total = jnp.zeros((SHARDS, 128), F32)
    wide_ids[...] = ids_ref[...].reshape(SHARDS, 16, ROWS).astype(F32)

    def both(row):
        return jnp.concatenate([wide_ids[:, row, :], wide_ids[:, row + 1, :]], axis=1)

    for table in range(2):
        mine = both(2 * table) == here
        rank = nn(jnp.where(mine, 1.0, 0.0).astype(BF16), before)
        local = both(2 * MICRO + 2 * table) + (1.0 + table * QROW_DEV)
        for k in range(CAP):
            value = jnp.where(mine & (rank == float(k)), local, 0.0)
            value = jnp.sum(value, axis=1, keepdims=True)
            total = total + jnp.where(lane == table * CAP + k, value, 0.0)
    slot = lax.broadcasted_iota(jnp.int32, (128, SLOTS), 1)
    spread = jnp.where(slot % (2 * CAP) == lax.broadcasted_iota(jnp.int32, (128, SLOTS), 0), 1.0, 0.0)
    wide = nn(total.astype(BF16), spread.astype(BF16))
    slot = lax.broadcasted_iota(jnp.int32, (SHARDS, SLOTS), 1)
    shard = lax.broadcasted_iota(jnp.int32, (SHARDS, SLOTS), 0)
    shard = shard % X_SIZE * Z_SIZE + shard // X_SIZE
    own = slot // (2 * CAP) == shard
    wide = jnp.sum(jnp.where(own, wide, 0.0), axis=0, keepdims=True)
    rows_ref[...] = wide.astype(jnp.int32) - 1


def relay_kernel(own_ref, *refs):
    got, (keep_ref, give_ref) = refs[:-2], refs[-2:]
    total = got[0][...]
    for one in got[1:]:
        total = total + one[...]
    total = jnp.where(lax.axis_index("section") == 0, own_ref[...], total)
    keep_ref[...] = total[:2 * ROWS]
    give_ref[...] = total[2 * ROWS:]


def send_kernel(slot_ref, keep_ref, got_ref, out_ref):
    own = keep_ref[...] + got_ref[...]
    place = lax.broadcasted_iota(jnp.int32, (SLOTS, ROWS), 0)
    total = None
    for m in range(MICRO):
        cols = slice(m * ROWS, (m + 1) * ROWS)
        hit = (place == slot_ref[0:1, cols]) | (place == slot_ref[1:2, cols])
        part = nt(jnp.where(hit, 1.0, 0.0).astype(BF16), own[cols, :])
        total = part if total is None else total + part
    out_ref[...] = total.astype(BF16)


def owner_kernel(rows_ref, arrived_ref, quot_ref, rem_ref):
    row = lax.broadcasted_iota(jnp.int32, (2 * QROW_DEV, SLOTS), 0)
    picks = jnp.where(row == rows_ref[...], 1.0, 0.0).astype(BF16)
    total = nn(picks, arrived_ref[...])
    quot_ref[...] = total[:QROW_DEV]
    rem_ref[...] = total[QROW_DEV:]


def shards(
    top_grad, layer_inputs, saved_pre, weight_in, weight_out, gain_in, gain_mid, lengths, quot_ids, rem_ids
):
    gain_t, *saved = forward(
        lengths.reshape(MICRO, 4), saved_pre[0], layer_inputs[0], top_grad, gain_mid, gain_in
    )
    *weights, ids = gather_weights(weight_in, weight_out, quot_ids, rem_ids)
    kept = [(*saved[4 * m:4 * m + 3], gain_t) for m in range(MICRO)]
    carried = [saved[4 * m + 3] for m in range(MICRO)]
    before, first = None, None
    for hop in range(SECTIONS):
        section = SECTIONS - 1 - hop
        for micro in range(MICRO):
            last = section == 0 and micro == 1
            extra = () if before is None else (before,)
            if section == 0 and micro == 0:
                extra = extra + (slots, rows)
            out = layer_step(
                section, carried[micro], first if last else None, kept[micro], weights, extra
            )
            if last:
                pieces = out
            elif section == 0:
                before = first = out
            else:
                before = out
                carried[micro] = lax.ppermute(out, "section", [(section, section - 1)])
        if section == 1:
            slots = pl.pallas_call(
                slots_kernel,
                in_specs=[VMEM, VMEM, HBM],
                out_specs=VMEM,
                out_shape=jax.ShapeDtypeStruct((2, MICRO * ROWS), jnp.int32),
                compiler_params=params(16),
                cost_estimate=cost(10**7, 8192),
                name="find_slots",
            )(quot_ids, rem_ids, before)
            rows = pl.pallas_call(
                rows_kernel,
                in_specs=[VMEM, HBM],
                out_specs=VMEM,
                out_shape=jax.ShapeDtypeStruct((1, SLOTS), jnp.int32),
                scratch_shapes=[pltpu.VMEM((SHARDS, 16, ROWS), F32)],
                compiler_params=params(32),
                cost_estimate=cost(3 * 10**7, MIB),
                name="find_rows",
            )(ids, before)

    got = [lax.ppermute(pieces[y], "section", [(0, 2 * y)]) for y in (2, 1, 3)]
    keep, give = pl.pallas_call(
        relay_kernel,
        in_specs=[VMEM] * 4,
        out_specs=[VMEM, VMEM],
        out_shape=[jax.ShapeDtypeStruct((2 * ROWS, ROWS), BF16)] * 2,
        compiler_params=params(16),
        cost_estimate=cost(10**6, MIB),
        name="relay",
    )(pieces[0], *got)
    give = lax.ppermute(give, "section", [(s, s + 1) for s in range(0, SECTIONS, 2)])
    send = pl.pallas_call(
        send_kernel,
        in_specs=[VMEM] * 3,
        out_specs=VMEM,
        out_shape=jax.ShapeDtypeStruct((SLOTS, 128), BF16),
        compiler_params=params(32),
        cost_estimate=cost(7 * 10**7, MIB),
        name="fill_slots",
    )(slots, keep, give)
    arrived = lax.all_to_all(
        send.reshape(SHARDS, 2 * CAP, 128), "shard", split_axis=0, concat_axis=0, tiled=True
    )
    return pl.pallas_call(
        owner_kernel,
        in_specs=[VMEM, VMEM],
        out_specs=[VMEM, VMEM],
        out_shape=[jax.ShapeDtypeStruct((QROW_DEV, 128), F32)] * 2,
        compiler_params=params(32),
        cost_estimate=cost(4 * 10**7, MIB),
        name="owner_sums",
    )(rows, arrived.reshape(SLOTS, 128))


def solution(mesh):
    placed = (
        P(None, "shard", None),
        P("section", None, "shard", None),
        P("section", None, "shard", None),
        P("section", "shard", None),
        P("section", "shard", None),
        P("section", None),
        P("section", None),
        P(None, "shard", None),
        P(None, "shard"),
        P(None, "shard"),
    )
    return jax.shard_map(
        shards,
        mesh=mesh,
        in_specs=placed,
        out_specs=(P("shard", "section"), P("shard", "section")),
        check_vma=False,
    )
```

```python
import functools
import math

import jax
import jax.numpy as jnp
from jax import lax
from jax.experimental import pallas as pl
from jax.experimental.pallas import tpu as pltpu
from jax.sharding import PartitionSpec as P

HEADS = 4
HEAD = 128
ATT = 512
ROWS = 128
WIDTH = 1024
SECTIONS = 8
MICRO = 2
SHARDS = 64
X_SIZE = 4
Z_SIZE = 16
QROW_DEV = 64
CAP = 8
SLOTS = SHARDS * 2 * CAP
EPSILON = 1e-05
BF16 = jnp.bfloat16
F32 = jnp.float32
MIB = 1024 * 1024
VMEM = pl.BlockSpec(memory_space=pltpu.VMEM)
HBM = pl.BlockSpec(memory_space=pl.ANY)

UGR, XHAT, EU, SV, SQ, SK, KT, QT, VN, AN, PT = range(11)
SAVED = 11


def nt(a, b):
    return lax.dot_general(a, b, (((1,), (1,)), ((), ())), preferred_element_type=F32)


def nn(a, b):
    return jnp.dot(a, b, preferred_element_type=F32)


def params(mib):
    return pltpu.CompilerParams(vmem_limit_bytes=mib * MIB)


def cost(flops, size):
    return pl.CostEstimate(flops=flops, bytes_accessed=size, transcendentals=0)


def segment_grid(len_ref, micro, dim):
    place = lax.broadcasted_iota(jnp.int32, (ROWS, ROWS), dim)
    end = jnp.int32(0)
    seg = jnp.zeros((ROWS, ROWS), jnp.int32)
    for k in range(4):
        end = end + len_ref[micro, k]
        seg = seg + (place >= end).astype(jnp.int32)
    return place, seg


def forward_kernel(len_ref, pre_hbm, x_hbm, top_hbm, gain_mid_ref, gain_in_ref, gain_t_ref, *refs):
    out_refs, (pre_ref, x_ref, top_ref, sems) = refs[:4 * MICRO], refs[4 * MICRO:]
    copies = []
    for k, (src, dst) in enumerate(((pre_hbm, pre_ref), (x_hbm, x_ref), (top_hbm, top_ref))):
        for micro in range(MICRO):
            copies.append(pltpu.make_async_copy(src.at[micro], dst.at[micro], sems.at[k, micro]))
            copies[-1].start()
    gain_t_ref[...] = jnp.broadcast_to(gain_in_ref[...], (ROWS, WIDTH)).T
    for one in copies:
        one.wait()
    for micro in range(MICRO):
        saved_ref, xh_ref, rstd_ref, top_t_ref = out_refs[4 * micro:4 * micro + 4]
        forward_part(len_ref, micro, pre_ref, x_ref, top_ref, gain_mid_ref[...],
                     saved_ref, xh_ref, rstd_ref, top_t_ref)


def forward_part(len_ref, micro, pre_ref, x_ref, top_ref, gain, saved_ref, xh_ref, rstd_ref, top_t_ref):
    def act(block):
        pre = pre_ref[micro, :, block * ATT:(block + 1) * ATT].astype(F32)
        sig = jax.nn.sigmoid(pre)
        return pre * sig, sig * (1.0 + pre * (1.0 - sig))

    row, seg_row = segment_grid(len_ref, micro, 0)
    col, seg_col = segment_grid(len_ref, micro, 1)
    same = seg_row == seg_col
    allowed = same & (col <= row)
    allowed_t = same & (row <= col)
    val, dval = act(1)
    que, dque = act(2)
    key, dkey = act(3)
    saved_ref[SV] = dval.T.astype(BF16)
    saved_ref[SQ] = dque.T.astype(BF16)
    saved_ref[SK] = dkey.T.astype(BF16)
    saved_ref[KT] = key.T.astype(BF16)
    saved_ref[QT] = que.T.astype(BF16)
    val, que, key = val.astype(BF16), que.astype(BF16), key.astype(BF16)
    scale = 1.0 / math.sqrt(HEAD)
    mixture = []
    for h in range(HEADS):
        cols = slice(h * HEAD, (h + 1) * HEAD)
        scores = nt(que[:, cols], key[:, cols]) * scale
        soft = jnp.where(allowed, scores * jax.nn.sigmoid(scores), 0.0).astype(BF16)
        scores = nt(key[:, cols], que[:, cols]) * scale
        sig = jax.nn.sigmoid(scores)
        slope = jnp.where(allowed_t, sig * (1.0 + scores * (1.0 - sig)) * scale, 0.0)
        saved_ref[VN, cols, :] = val[:, cols]
        saved_ref[AN, cols, :] = soft
        saved_ref[PT, cols, :] = slope.astype(BF16)
        mixture.append(nn(soft, val[:, cols]))
    mixture = jnp.concatenate(mixture, axis=1)
    centred = mixture - jnp.mean(mixture, axis=1, keepdims=True)
    rstd = lax.rsqrt(jnp.mean(centred * centred, axis=1, keepdims=True) + EPSILON)
    xhat = centred * rstd
    gate, dgate = act(0)
    saved_ref[UGR] = (gate * gain * rstd).T.astype(BF16)
    saved_ref[XHAT] = xhat.T.astype(BF16)
    saved_ref[EU] = (xhat * gain * dgate).T.astype(BF16)
    x = x_ref[micro].astype(F32).T
    x = x - jnp.mean(x, axis=0, keepdims=True)
    rstd = lax.rsqrt(jnp.mean(x * x, axis=0, keepdims=True) + EPSILON)
    xh_ref[...] = (x * rstd).astype(BF16)
    rstd_ref[...] = jnp.broadcast_to(rstd, (8, ROWS))
    top_t_ref[...] = top_ref[micro].astype(F32).T.astype(BF16)


def forward(lengths, pre, x, top, gain_mid, gain_in):
    smem = pl.BlockSpec(memory_space=pltpu.SMEM)
    tall = jax.ShapeDtypeStruct((WIDTH, ROWS), BF16)
    each = [
        jax.ShapeDtypeStruct((SAVED, ATT, ROWS), BF16),
        tall,
        jax.ShapeDtypeStruct((8, ROWS), F32),
        tall,
    ]
    return pl.pallas_call(
        forward_kernel,
        in_specs=[smem] + [pl.BlockSpec(memory_space=pltpu.HBM)] * 3 + [VMEM] * 2,
        out_specs=[VMEM] * 9,
        out_shape=[jax.ShapeDtypeStruct((WIDTH, ROWS), F32)] + each * MICRO,
        scratch_shapes=[
            pltpu.VMEM((MICRO, ROWS, 4 * ATT), BF16),
            pltpu.VMEM((MICRO, ROWS, WIDTH), BF16),
            pltpu.VMEM((MICRO, ROWS, WIDTH), BF16),
            pltpu.SemaphoreType.DMA((3, MICRO)),
        ],
        compiler_params=params(32),
        cost_estimate=cost(2 * 10**8, 6 * MIB),
        name="saved_parts",
    )(lengths, pre, x, top, gain_mid, gain_in)


HALVES = 2048
LINE = HALVES + 512


def join_kernel(w_in_ref, w_out_ref, out_ref):
    out_ref[:, :HALVES] = w_in_ref[0]
    wide = w_out_ref[0].astype(F32)
    halves = jnp.concatenate([wide[:, :512], wide[:, 512:]], axis=0)
    out_ref[:, HALVES:] = halves.astype(BF16)


def pair_kernel(own_ref, next_ref, out_ref):
    rows = own_ref.shape[0]
    out_ref[:rows, :] = own_ref[...]
    out_ref[rows:, :] = next_ref[...]


def pair(own, other):
    return pl.pallas_call(
        pair_kernel,
        in_specs=[VMEM, VMEM],
        out_specs=VMEM,
        out_shape=jax.ShapeDtypeStruct((2 * own.shape[0], LINE), BF16),
        compiler_params=params(16),
        cost_estimate=cost(1000, 4 * own.shape[0] * LINE * 2),
        name="pair_weights",
    )(own, other)


def along(value, dx, dz):
    pairs = []
    for x in range(X_SIZE):
        for z in range(Z_SIZE):
            to = (x + dx) % X_SIZE * Z_SIZE + (z + dz) % Z_SIZE
            pairs.append((x * Z_SIZE + z, to))
    return lax.ppermute(value, "shard", pairs)


def gather_weights(weight_in, weight_out):
    own = pl.pallas_call(
        join_kernel,
        in_specs=[VMEM] * 2,
        out_specs=VMEM,
        out_shape=jax.ShapeDtypeStruct((16, LINE), BF16),
        compiler_params=params(16),
        cost_estimate=cost(1000, 160 * 1024),
        name="join_weights",
    )(weight_in, weight_out)
    block = pair(own, along(own, -1, 0))
    block = pair(block, along(block, -2, 0))
    blocks, offsets = [block], [0]
    up = down = block
    half = Z_SIZE // 2
    for hop in range(1, half + 1):
        up = along(up, 0, 1)
        blocks.append(up)
        offsets.append(-hop)
        if hop < half:
            down = along(down, 0, -1)
            blocks.append(down)
            offsets.append(hop)
    return pl.pallas_call(
        functools.partial(place_kernel, tuple(offsets)),
        in_specs=[VMEM] * Z_SIZE,
        out_specs=[VMEM] * 2,
        out_shape=[
            jax.ShapeDtypeStruct((Z_SIZE, 64, 2048), BF16),
            jax.ShapeDtypeStruct((Z_SIZE, 16, 2048), BF16),
        ],
        scratch_shapes=[pltpu.VMEM((Z_SIZE, 32, 1024), F32)],
        compiler_params=params(32),
        cost_estimate=cost(1000, 10 * MIB),
        name="place_weights",
    )(*blocks)


def place_kernel(offsets, *refs):
    blocks, (w_in_ref, w_out_ref, wide) = refs[:Z_SIZE], refs[Z_SIZE:]
    here_x = lax.axis_index("shard") // Z_SIZE
    here_z = lax.axis_index("shard") % Z_SIZE
    for block, offset in zip(blocks, offsets):
        z = (here_z + Z_SIZE + offset) % Z_SIZE
        for step in range(X_SIZE):
            x = (here_x + step) % X_SIZE
            rows = slice(step * 16, (step + 1) * 16)
            w_in_ref[z, pl.ds(pl.multiple_of(x * 16, 16), 16), :] = block[rows, :HALVES]
            halves = block[rows, HALVES:].astype(F32)
            at = pl.ds(pl.multiple_of(x * 8, 8), 8)
            wide[z, at, 0:512] = halves[0:8]
            wide[z, at, 512:1024] = halves[8:16]
    for z in range(Z_SIZE):
        w_out_ref[z, :, 0:1024] = wide[z, 0:16, :].astype(BF16)
        w_out_ref[z, :, 1024:2048] = wide[z, 16:32, :].astype(BF16)


def step_kernel(at_section, last, n_extra, *refs):
    refs = list(refs)
    g_ref = refs.pop(0)
    first_ref = refs.pop(0) if last else None
    saved, xh, rstd, gain, w_in, w_out = refs[:6]
    outs, gp = refs[6 + n_extra:-1], refs[-1]

    @pl.when(lax.axis_index("section") == at_section)
    def _():
        grad = g_ref[...]
        grad_mid = []
        for half in range(2):
            weight = w_out[:, :, half * 1024:(half + 1) * 1024].reshape(256, 1024)
            both = nn(weight, grad).reshape(Z_SIZE, 2, 8, ROWS)
            grad_mid += [both[:, 0].reshape(HEAD, ROWS), both[:, 1].reshape(HEAD, ROWS)]

        def part(name, h):
            return saved[name, h * HEAD:(h + 1) * HEAD, :]

        terms = [grad_mid[h] * part(UGR, h).astype(F32) for h in range(HEADS)]
        xhats = [part(XHAT, h).astype(F32) for h in range(HEADS)]
        mean_1 = sum(terms[1:], terms[0])
        mean_2 = terms[0] * xhats[0]
        for h in range(1, HEADS):
            mean_2 = mean_2 + terms[h] * xhats[h]
        mean_1 = jnp.sum(mean_1, axis=0, keepdims=True) * (1.0 / ATT)
        mean_2 = jnp.sum(mean_2, axis=0, keepdims=True) * (1.0 / ATT)
        for h in range(HEADS):
            def put(block, value):
                start = block * ATT + h * HEAD
                gp[start:start + HEAD, :] = value.astype(BF16)

            put(0, grad_mid[h] * part(EU, h).astype(F32))
            d_o = (terms[h] - mean_1 - xhats[h] * mean_2).astype(BF16)
            d_s = (nn(part(VN, h), d_o) * part(PT, h).astype(F32)).astype(BF16)
            put(1, nn(d_o, part(AN, h)) * part(SV, h).astype(F32))
            put(2, nn(part(KT, h), d_s) * part(SQ, h).astype(F32))
            put(3, nt(part(QT, h), d_s) * part(SK, h).astype(F32))
        product = nn(w_in[...].reshape(WIDTH, 4 * ATT), gp[...])
        product = product.reshape(Z_SIZE, X_SIZE, 16, ROWS)
        d_xh, x_hat = [], []
        for x in range(X_SIZE):
            rows = slice(x * 256, (x + 1) * 256)
            d_xh.append(product[:, x].reshape(256, ROWS) * gain[rows, :])
            x_hat.append(xh[rows, :].astype(F32))
        mean_1 = sum(d_xh[1:], d_xh[0])
        mean_2 = d_xh[0] * x_hat[0]
        for x in range(1, X_SIZE):
            mean_2 = mean_2 + d_xh[x] * x_hat[x]
        mean_1 = jnp.sum(mean_1, axis=0, keepdims=True) * (1.0 / WIDTH)
        mean_2 = jnp.sum(mean_2, axis=0, keepdims=True) * (1.0 / WIDTH)
        scale = rstd[0:1, :]
        for x in range(X_SIZE):
            rows = slice(x * 256, (x + 1) * 256)
            d_x = (d_xh[x] - mean_1 - x_hat[x] * mean_2) * scale
            result = (grad[rows, :].astype(F32) + d_x).astype(BF16)
            if last:
                outs[x][ROWS:2 * ROWS, :] = result[0:128]
                outs[x][3 * ROWS:, :] = result[128:256]
            else:
                outs[0][rows, :] = result
        if last:
            for x in range(X_SIZE):
                outs[x][0:ROWS, :] = first_ref[x * 256:x * 256 + 128, :]
                outs[x][2 * ROWS:3 * ROWS, :] = first_ref[x * 256 + 128:(x + 1) * 256, :]


def layer_step(at_section, grad, first, kept, weights, extra):
    last = first is not None
    operands = [grad, first] if last else [grad]
    operands += [*kept, *weights]
    if last:
        out_shape = [jax.ShapeDtypeStruct((4 * ROWS, ROWS), BF16)] * (SECTIONS // 2)
    else:
        out_shape = [jax.ShapeDtypeStruct((WIDTH, ROWS), BF16)]
    out = pl.pallas_call(
        functools.partial(step_kernel, at_section, last, len(extra)),
        in_specs=[VMEM] * len(operands) + [HBM] * len(extra),
        out_specs=[VMEM] * len(out_shape),
        out_shape=out_shape,
        scratch_shapes=[pltpu.VMEM((4 * ATT, ROWS), BF16)],
        compiler_params=params(32),
        cost_estimate=cost(7 * 10**8, 8 * MIB),
        name="layer_step",
    )(*operands, *extra)
    return out if last else out[0]


def slots_kernel(quot_ref, rem_ref, _, slot_ref, rows_ref):
    tokens = MICRO * ROWS
    owners = lax.broadcasted_iota(jnp.int32, (SHARDS, tokens), 0)
    before = (
        lax.broadcasted_iota(jnp.int32, (tokens, tokens), 0)
        < lax.broadcasted_iota(jnp.int32, (tokens, tokens), 1)
    )
    before = jnp.where(before, 1.0, 0.0).astype(BF16)
    place = lax.broadcasted_iota(jnp.int32, (2 * CAP, tokens), 0)
    total = jnp.zeros((SHARDS, 2 * CAP), F32)
    for table, ref in enumerate((quot_ref, rem_ref)):
        ids = jnp.concatenate([ref[0:1, :], ref[1:2, :]], axis=1)
        owner = lax.shift_right_logical(ids, 6)
        local = ids - owner * QROW_DEV + (1 + table * QROW_DEV)
        match = owners == owner
        one_hot = jnp.where(match, 1.0, 0.0)
        earlier = nn(one_hot.astype(BF16), before)
        rank = jnp.sum(earlier * one_hot, axis=0, keepdims=True).astype(jnp.int32)
        rank = rank + table * CAP
        slot_ref[table:table + 1, :] = owner * (2 * CAP) + rank
        values = jnp.where(match, local.astype(F32), 0.0).astype(BF16)
        total = total + nt(values, jnp.where(place == rank, 1.0, 0.0).astype(BF16))
    rows_ref[...] = total.astype(jnp.int32) - 1


def relay_kernel(own_ref, *refs):
    got, (keep_ref, give_ref) = refs[:-2], refs[-2:]
    total = got[0][...]
    for one in got[1:]:
        total = total + one[...]
    total = jnp.where(lax.axis_index("section") == 0, own_ref[...], total)
    keep_ref[...] = total[:2 * ROWS]
    give_ref[...] = total[2 * ROWS:]


def send_kernel(slot_ref, keep_ref, got_ref, out_ref):
    own = keep_ref[...] + got_ref[...]
    place = lax.broadcasted_iota(jnp.int32, (SLOTS, ROWS), 0)
    total = None
    for m in range(MICRO):
        cols = slice(m * ROWS, (m + 1) * ROWS)
        hit = (place == slot_ref[0:1, cols]) | (place == slot_ref[1:2, cols])
        part = nt(jnp.where(hit, 1.0, 0.0).astype(BF16), own[cols, :])
        total = part if total is None else total + part
    out_ref[...] = total.astype(BF16)


def owner_kernel(rows_ref, arrived_ref, quot_ref, rem_ref):
    row = lax.broadcasted_iota(jnp.int32, (2 * QROW_DEV, SLOTS), 0)
    picks = jnp.where(row == rows_ref[...], 1.0, 0.0).astype(BF16)
    total = nn(picks, arrived_ref[...])
    quot_ref[...] = total[:QROW_DEV]
    rem_ref[...] = total[QROW_DEV:]


def shards(
    top_grad, layer_inputs, saved_pre, weight_in, weight_out, gain_in, gain_mid, lengths, quot_ids, rem_ids
):
    gain_t, *saved = forward(
        lengths.reshape(MICRO, 4), saved_pre[0], layer_inputs[0], top_grad, gain_mid, gain_in
    )
    weights = gather_weights(weight_in, weight_out)
    kept = [(*saved[4 * m:4 * m + 3], gain_t) for m in range(MICRO)]
    carried = [saved[4 * m + 3] for m in range(MICRO)]
    before, first = None, None
    for hop in range(SECTIONS):
        section = SECTIONS - 1 - hop
        for micro in range(MICRO):
            last = section == 0 and micro == 1
            extra = () if before is None else (before,)
            if section == 1 and micro == 0:
                extra = extra + (slots, rows)
            out = layer_step(
                section, carried[micro], first if last else None, kept[micro], weights, extra
            )
            if last:
                pieces = out
            elif section == 0:
                before = first = out
            else:
                before = out
                carried[micro] = lax.ppermute(out, "section", [(section, section - 1)])
        if section == 2:
            slots, rows = pl.pallas_call(
                slots_kernel,
                in_specs=[VMEM, VMEM, HBM],
                out_specs=[VMEM, VMEM],
                out_shape=[
                    jax.ShapeDtypeStruct((2, MICRO * ROWS), jnp.int32),
                    jax.ShapeDtypeStruct((SHARDS, 2 * CAP), jnp.int32),
                ],
                compiler_params=params(16),
                cost_estimate=cost(10**7, 8192),
                name="find_slots",
            )(quot_ids, rem_ids, before)
            rows = lax.all_to_all(
                rows.reshape(SHARDS, 1, 2 * CAP), "shard", split_axis=0, concat_axis=0, tiled=True
            ).reshape(1, SLOTS)

    got = [lax.ppermute(pieces[y], "section", [(0, 2 * y)]) for y in (2, 1, 3)]
    keep, give = pl.pallas_call(
        relay_kernel,
        in_specs=[VMEM] * 4,
        out_specs=[VMEM, VMEM],
        out_shape=[jax.ShapeDtypeStruct((2 * ROWS, ROWS), BF16)] * 2,
        compiler_params=params(16),
        cost_estimate=cost(10**6, MIB),
        name="relay",
    )(pieces[0], *got)
    give = lax.ppermute(give, "section", [(s, s + 1) for s in range(0, SECTIONS, 2)])
    send = pl.pallas_call(
        send_kernel,
        in_specs=[VMEM] * 3,
        out_specs=VMEM,
        out_shape=jax.ShapeDtypeStruct((SLOTS, 128), BF16),
        compiler_params=params(32),
        cost_estimate=cost(7 * 10**7, MIB),
        name="fill_slots",
    )(slots, keep, give)
    arrived = lax.all_to_all(
        send.reshape(SHARDS, 2 * CAP, 128), "shard", split_axis=0, concat_axis=0, tiled=True
    )
    return pl.pallas_call(
        owner_kernel,
        in_specs=[VMEM, VMEM],
        out_specs=[VMEM, VMEM],
        out_shape=[jax.ShapeDtypeStruct((QROW_DEV, 128), F32)] * 2,
        compiler_params=params(32),
        cost_estimate=cost(4 * 10**7, MIB),
        name="owner_sums",
    )(rows, arrived.reshape(SLOTS, 128))


def solution(mesh):
    placed = (
        P(None, "shard", None),
        P("section", None, "shard", None),
        P("section", None, "shard", None),
        P("section", "shard", None),
        P("section", "shard", None),
        P("section", None),
        P("section", None),
        P(None, "shard", None),
        P(None, "shard"),
        P(None, "shard"),
    )
    return jax.shard_map(
        shards,
        mesh=mesh,
        in_specs=placed,
        out_specs=(P("shard", "section"), P("shard", "section")),
        check_vma=False,
    )
```

```python
import functools
import math

import jax
import jax.numpy as jnp
from jax import lax
from jax.experimental import pallas as pl
from jax.experimental.pallas import tpu as pltpu
from jax.sharding import PartitionSpec as P

HEADS = 4
HEAD = 128
ATT = 512
ROWS = 128
WIDTH = 1024
SECTIONS = 8
MICRO = 2
SHARDS = 64
X_SIZE = 4
Z_SIZE = 16
QROW_DEV = 64
CAP = 8
SLOTS = SHARDS * 2 * CAP
EPSILON = 1e-05
BF16 = jnp.bfloat16
F32 = jnp.float32
MIB = 1024 * 1024
VMEM = pl.BlockSpec(memory_space=pltpu.VMEM)
HBM = pl.BlockSpec(memory_space=pl.ANY)

UGR, XHAT, EU, SV, SQ, SK, KT, QT, VN, AN, PT = range(11)
SAVED = 11


def nt(a, b):
    return lax.dot_general(a, b, (((1,), (1,)), ((), ())), preferred_element_type=F32)


def nn(a, b):
    return jnp.dot(a, b, preferred_element_type=F32)


def params(mib):
    return pltpu.CompilerParams(vmem_limit_bytes=mib * MIB)


def cost(flops, size):
    return pl.CostEstimate(flops=flops, bytes_accessed=size, transcendentals=0)


def segment_grid(len_ref, micro, dim):
    place = lax.broadcasted_iota(jnp.int32, (ROWS, ROWS), dim)
    end = jnp.int32(0)
    seg = jnp.zeros((ROWS, ROWS), jnp.int32)
    for k in range(4):
        end = end + len_ref[micro, k]
        seg = seg + (place >= end).astype(jnp.int32)
    return place, seg


def forward_kernel(len_ref, pre_hbm, x_hbm, top_hbm, gain_mid_ref, gain_in_ref, gain_t_ref, *refs):
    out_refs, (pre_ref, x_ref, top_ref, sems) = refs[:4 * MICRO], refs[4 * MICRO:]
    copies = []
    for k, (src, dst) in enumerate(((pre_hbm, pre_ref), (x_hbm, x_ref), (top_hbm, top_ref))):
        for micro in range(MICRO):
            copies.append(pltpu.make_async_copy(src.at[micro], dst.at[micro], sems.at[k, micro]))
            copies[-1].start()
    gain_t_ref[...] = jnp.broadcast_to(gain_in_ref[...], (ROWS, WIDTH)).T
    for one in copies:
        one.wait()
    for micro in range(MICRO):
        saved_ref, xh_ref, rstd_ref, top_t_ref = out_refs[4 * micro:4 * micro + 4]
        forward_part(len_ref, micro, pre_ref, x_ref, top_ref, gain_mid_ref[...],
                     saved_ref, xh_ref, rstd_ref, top_t_ref)


def forward_part(len_ref, micro, pre_ref, x_ref, top_ref, gain, saved_ref, xh_ref, rstd_ref, top_t_ref):
    def act(block):
        pre = pre_ref[micro, :, block * ATT:(block + 1) * ATT].astype(F32)
        sig = jax.nn.sigmoid(pre)
        return pre * sig, sig * (1.0 + pre * (1.0 - sig))

    row, seg_row = segment_grid(len_ref, micro, 0)
    col, seg_col = segment_grid(len_ref, micro, 1)
    same = seg_row == seg_col
    allowed = same & (col <= row)
    allowed_t = same & (row <= col)
    val, dval = act(1)
    que, dque = act(2)
    key, dkey = act(3)
    saved_ref[SV] = dval.T.astype(BF16)
    saved_ref[SQ] = dque.T.astype(BF16)
    saved_ref[SK] = dkey.T.astype(BF16)
    saved_ref[KT] = key.T.astype(BF16)
    saved_ref[QT] = que.T.astype(BF16)
    val, que, key = val.astype(BF16), que.astype(BF16), key.astype(BF16)
    scale = 1.0 / math.sqrt(HEAD)
    mixture = []
    for h in range(HEADS):
        cols = slice(h * HEAD, (h + 1) * HEAD)
        scores = nt(que[:, cols], key[:, cols]) * scale
        soft = jnp.where(allowed, scores * jax.nn.sigmoid(scores), 0.0).astype(BF16)
        scores = nt(key[:, cols], que[:, cols]) * scale
        sig = jax.nn.sigmoid(scores)
        slope = jnp.where(allowed_t, sig * (1.0 + scores * (1.0 - sig)) * scale, 0.0)
        saved_ref[VN, cols, :] = val[:, cols]
        saved_ref[AN, cols, :] = soft
        saved_ref[PT, cols, :] = slope.astype(BF16)
        mixture.append(nn(soft, val[:, cols]))
    mixture = jnp.concatenate(mixture, axis=1)
    centred = mixture - jnp.mean(mixture, axis=1, keepdims=True)
    rstd = lax.rsqrt(jnp.mean(centred * centred, axis=1, keepdims=True) + EPSILON)
    xhat = centred * rstd
    gate, dgate = act(0)
    saved_ref[UGR] = (gate * gain * rstd).T.astype(BF16)
    saved_ref[XHAT] = xhat.T.astype(BF16)
    saved_ref[EU] = (xhat * gain * dgate).T.astype(BF16)
    x = x_ref[micro].astype(F32).T
    x = x - jnp.mean(x, axis=0, keepdims=True)
    rstd = lax.rsqrt(jnp.mean(x * x, axis=0, keepdims=True) + EPSILON)
    xh_ref[...] = (x * rstd).astype(BF16)
    rstd_ref[...] = jnp.broadcast_to(rstd, (8, ROWS))
    top_t_ref[...] = top_ref[micro].astype(F32).T.astype(BF16)


def forward(lengths, pre, x, top, gain_mid, gain_in):
    smem = pl.BlockSpec(memory_space=pltpu.SMEM)
    tall = jax.ShapeDtypeStruct((WIDTH, ROWS), BF16)
    each = [
        jax.ShapeDtypeStruct((SAVED, ATT, ROWS), BF16),
        tall,
        jax.ShapeDtypeStruct((8, ROWS), F32),
        tall,
    ]
    return pl.pallas_call(
        forward_kernel,
        in_specs=[smem] + [pl.BlockSpec(memory_space=pltpu.HBM)] * 3 + [VMEM] * 2,
        out_specs=[VMEM] * 9,
        out_shape=[jax.ShapeDtypeStruct((WIDTH, ROWS), F32)] + each * MICRO,
        scratch_shapes=[
            pltpu.VMEM((MICRO, ROWS, 4 * ATT), BF16),
            pltpu.VMEM((MICRO, ROWS, WIDTH), BF16),
            pltpu.VMEM((MICRO, ROWS, WIDTH), BF16),
            pltpu.SemaphoreType.DMA((3, MICRO)),
        ],
        compiler_params=params(32),
        cost_estimate=cost(2 * 10**8, 6 * MIB),
        name="saved_parts",
    )(lengths, pre, x, top, gain_mid, gain_in)


HALVES = 2048
IDS = HALVES + 512
LINE = IDS + ROWS


def join_kernel(w_in_ref, w_out_ref, quot_ref, rem_ref, out_ref):
    out_ref[:, :HALVES] = w_in_ref[0]
    wide = w_out_ref[0].astype(F32)
    halves = jnp.concatenate([wide[:, :512], wide[:, 512:]], axis=0)
    out_ref[:, HALVES:IDS] = halves.astype(BF16)
    ids = jnp.concatenate([quot_ref[...], rem_ref[...]], axis=0)
    owner = lax.shift_right_logical(ids, 6)
    local = ids - owner * QROW_DEV
    blank = jnp.zeros((8, ROWS), F32)
    coded = jnp.concatenate([owner.astype(F32), local.astype(F32), blank], axis=0)
    out_ref[:, IDS:] = coded.astype(BF16)


def pair_kernel(own_ref, next_ref, out_ref):
    rows = own_ref.shape[0]
    out_ref[:rows, :] = own_ref[...]
    out_ref[rows:, :] = next_ref[...]


def pair(own, other):
    return pl.pallas_call(
        pair_kernel,
        in_specs=[VMEM, VMEM],
        out_specs=VMEM,
        out_shape=jax.ShapeDtypeStruct((2 * own.shape[0], LINE), BF16),
        compiler_params=params(16),
        cost_estimate=cost(1000, 4 * own.shape[0] * LINE * 2),
        name="pair_weights",
    )(own, other)


def along(value, dx, dz):
    pairs = []
    for x in range(X_SIZE):
        for z in range(Z_SIZE):
            to = (x + dx) % X_SIZE * Z_SIZE + (z + dz) % Z_SIZE
            pairs.append((x * Z_SIZE + z, to))
    return lax.ppermute(value, "shard", pairs)


def gather_weights(weight_in, weight_out, quot_ids, rem_ids):
    own = pl.pallas_call(
        join_kernel,
        in_specs=[VMEM] * 4,
        out_specs=VMEM,
        out_shape=jax.ShapeDtypeStruct((16, LINE), BF16),
        compiler_params=params(16),
        cost_estimate=cost(1000, 160 * 1024),
        name="join_weights",
    )(weight_in, weight_out, quot_ids, rem_ids)
    block = pair(own, along(own, -1, 0))
    block = pair(block, along(block, -2, 0))
    blocks, offsets = [block], [0]
    up = down = block
    half = Z_SIZE // 2
    for hop in range(1, half + 1):
        up = along(up, 0, 1)
        blocks.append(up)
        offsets.append(-hop)
        if hop < half:
            down = along(down, 0, -1)
            blocks.append(down)
            offsets.append(hop)
    return pl.pallas_call(
        functools.partial(place_kernel, tuple(offsets)),
        in_specs=[VMEM] * Z_SIZE,
        out_specs=[VMEM] * 3,
        out_shape=[
            jax.ShapeDtypeStruct((Z_SIZE, 64, 2048), BF16),
            jax.ShapeDtypeStruct((Z_SIZE, 16, 2048), BF16),
            jax.ShapeDtypeStruct((Z_SIZE, X_SIZE, 16, ROWS), BF16),
        ],
        scratch_shapes=[pltpu.VMEM((Z_SIZE, 32, 1024), F32)],
        compiler_params=params(32),
        cost_estimate=cost(1000, 10 * MIB),
        name="place_weights",
    )(*blocks)


def place_kernel(offsets, *refs):
    blocks, (w_in_ref, w_out_ref, ids_ref, wide) = refs[:Z_SIZE], refs[Z_SIZE:]
    here_x = lax.axis_index("shard") // Z_SIZE
    here_z = lax.axis_index("shard") % Z_SIZE
    for block, offset in zip(blocks, offsets):
        z = (here_z + Z_SIZE + offset) % Z_SIZE
        for step in range(X_SIZE):
            x = (here_x + step) % X_SIZE
            rows = slice(step * 16, (step + 1) * 16)
            w_in_ref[z, pl.ds(pl.multiple_of(x * 16, 16), 16), :] = block[rows, :HALVES]
            ids_ref[z, x] = block[rows, IDS:]
            halves = block[rows, HALVES:IDS].astype(F32)
            at = pl.ds(pl.multiple_of(x * 8, 8), 8)
            wide[z, at, 0:512] = halves[0:8]
            wide[z, at, 512:1024] = halves[8:16]
    for z in range(Z_SIZE):
        w_out_ref[z, :, 0:1024] = wide[z, 0:16, :].astype(BF16)
        w_out_ref[z, :, 1024:2048] = wide[z, 16:32, :].astype(BF16)


def step_kernel(at_section, last, n_extra, *refs):
    refs = list(refs)
    g_ref = refs.pop(0)
    first_ref = refs.pop(0) if last else None
    saved, xh, rstd, gain, w_in, w_out = refs[:6]
    outs, gp = refs[6 + n_extra:-1], refs[-1]

    @pl.when(lax.axis_index("section") == at_section)
    def _():
        grad = g_ref[...]
        grad_mid = []
        for half in range(2):
            weight = w_out[:, :, half * 1024:(half + 1) * 1024].reshape(256, 1024)
            both = nn(weight, grad).reshape(Z_SIZE, 2, 8, ROWS)
            grad_mid += [both[:, 0].reshape(HEAD, ROWS), both[:, 1].reshape(HEAD, ROWS)]

        def part(name, h):
            return saved[name, h * HEAD:(h + 1) * HEAD, :]

        terms = [grad_mid[h] * part(UGR, h).astype(F32) for h in range(HEADS)]
        xhats = [part(XHAT, h).astype(F32) for h in range(HEADS)]
        mean_1 = sum(terms[1:], terms[0])
        mean_2 = terms[0] * xhats[0]
        for h in range(1, HEADS):
            mean_2 = mean_2 + terms[h] * xhats[h]
        mean_1 = jnp.sum(mean_1, axis=0, keepdims=True) * (1.0 / ATT)
        mean_2 = jnp.sum(mean_2, axis=0, keepdims=True) * (1.0 / ATT)
        for h in range(HEADS):
            def put(block, value):
                start = block * ATT + h * HEAD
                gp[start:start + HEAD, :] = value.astype(BF16)

            put(0, grad_mid[h] * part(EU, h).astype(F32))
            d_o = (terms[h] - mean_1 - xhats[h] * mean_2).astype(BF16)
            d_s = (nn(part(VN, h), d_o) * part(PT, h).astype(F32)).astype(BF16)
            put(1, nn(d_o, part(AN, h)) * part(SV, h).astype(F32))
            put(2, nn(part(KT, h), d_s) * part(SQ, h).astype(F32))
            put(3, nt(part(QT, h), d_s) * part(SK, h).astype(F32))
        product = nn(w_in[...].reshape(WIDTH, 4 * ATT), gp[...])
        product = product.reshape(Z_SIZE, X_SIZE, 16, ROWS)
        d_xh, x_hat = [], []
        for x in range(X_SIZE):
            rows = slice(x * 256, (x + 1) * 256)
            d_xh.append(product[:, x].reshape(256, ROWS) * gain[rows, :])
            x_hat.append(xh[rows, :].astype(F32))
        mean_1 = sum(d_xh[1:], d_xh[0])
        mean_2 = d_xh[0] * x_hat[0]
        for x in range(1, X_SIZE):
            mean_2 = mean_2 + d_xh[x] * x_hat[x]
        mean_1 = jnp.sum(mean_1, axis=0, keepdims=True) * (1.0 / WIDTH)
        mean_2 = jnp.sum(mean_2, axis=0, keepdims=True) * (1.0 / WIDTH)
        scale = rstd[0:1, :]
        for x in range(X_SIZE):
            rows = slice(x * 256, (x + 1) * 256)
            d_x = (d_xh[x] - mean_1 - x_hat[x] * mean_2) * scale
            result = (grad[rows, :].astype(F32) + d_x).astype(BF16)
            if last:
                outs[x][ROWS:2 * ROWS, :] = result[0:128]
                outs[x][3 * ROWS:, :] = result[128:256]
            else:
                outs[0][rows, :] = result
        if last:
            for x in range(X_SIZE):
                outs[x][0:ROWS, :] = first_ref[x * 256:x * 256 + 128, :]
                outs[x][2 * ROWS:3 * ROWS, :] = first_ref[x * 256 + 128:(x + 1) * 256, :]


def layer_step(at_section, grad, first, kept, weights, extra):
    last = first is not None
    operands = [grad, first] if last else [grad]
    operands += [*kept, *weights]
    if last:
        out_shape = [jax.ShapeDtypeStruct((4 * ROWS, ROWS), BF16)] * (SECTIONS // 2)
    else:
        out_shape = [jax.ShapeDtypeStruct((WIDTH, ROWS), BF16)]
    out = pl.pallas_call(
        functools.partial(step_kernel, at_section, last, len(extra)),
        in_specs=[VMEM] * len(operands) + [HBM] * len(extra),
        out_specs=[VMEM] * len(out_shape),
        out_shape=out_shape,
        scratch_shapes=[pltpu.VMEM((4 * ATT, ROWS), BF16)],
        compiler_params=params(32),
        cost_estimate=cost(7 * 10**8, 8 * MIB),
        name="layer_step",
    )(*operands, *extra)
    return out if last else out[0]


def earlier_mask():
    tokens = MICRO * ROWS
    before = (
        lax.broadcasted_iota(jnp.int32, (tokens, tokens), 0)
        < lax.broadcasted_iota(jnp.int32, (tokens, tokens), 1)
    )
    return jnp.where(before, 1.0, 0.0).astype(BF16)


def slots_kernel(quot_ref, rem_ref, _, slot_ref):
    owners = lax.broadcasted_iota(jnp.int32, (SHARDS, MICRO * ROWS), 0)
    before = earlier_mask()
    for table, ref in enumerate((quot_ref, rem_ref)):
        ids = jnp.concatenate([ref[0:1, :], ref[1:2, :]], axis=1)
        owner = lax.shift_right_logical(ids, 6)
        one_hot = jnp.where(owners == owner, 1.0, 0.0)
        earlier = nn(one_hot.astype(BF16), before)
        rank = jnp.sum(earlier * one_hot, axis=0, keepdims=True).astype(jnp.int32)
        slot_ref[table:table + 1, :] = owner * (2 * CAP) + rank + table * CAP


def rows_kernel(ids_ref, _, rows_ref, wide_ids):
    here = lax.axis_index("shard").astype(F32)
    before = earlier_mask()
    lane = lax.broadcasted_iota(jnp.int32, (SHARDS, 128), 1)
    total = jnp.zeros((SHARDS, 128), F32)
    wide_ids[...] = ids_ref[...].reshape(SHARDS, 16, ROWS).astype(F32)

    def both(row):
        return jnp.concatenate([wide_ids[:, row, :], wide_ids[:, row + 1, :]], axis=1)

    for table in range(2):
        mine = both(2 * table) == here
        rank = nn(jnp.where(mine, 1.0, 0.0).astype(BF16), before)
        local = both(2 * MICRO + 2 * table) + (1.0 + table * QROW_DEV)
        for k in range(CAP):
            value = jnp.where(mine & (rank == float(k)), local, 0.0)
            value = jnp.sum(value, axis=1, keepdims=True)
            total = total + jnp.where(lane == table * CAP + k, value, 0.0)
    slot = lax.broadcasted_iota(jnp.int32, (128, SLOTS), 1)
    spread = jnp.where(slot % (2 * CAP) == lax.broadcasted_iota(jnp.int32, (128, SLOTS), 0), 1.0, 0.0)
    wide = nn(total.astype(BF16), spread.astype(BF16))
    slot = lax.broadcasted_iota(jnp.int32, (SHARDS, SLOTS), 1)
    shard = lax.broadcasted_iota(jnp.int32, (SHARDS, SLOTS), 0)
    shard = shard % X_SIZE * Z_SIZE + shard // X_SIZE
    own = slot // (2 * CAP) == shard
    wide = jnp.sum(jnp.where(own, wide, 0.0), axis=0, keepdims=True)
    rows_ref[...] = wide.astype(jnp.int32) - 1


def relay_kernel(own_ref, *refs):
    got, (keep_ref, give_ref) = refs[:-2], refs[-2:]
    total = got[0][...]
    for one in got[1:]:
        total = total + one[...]
    total = jnp.where(lax.axis_index("section") == 0, own_ref[...], total)
    keep_ref[...] = total[:2 * ROWS]
    give_ref[...] = total[2 * ROWS:]


def send_kernel(slot_ref, keep_ref, got_ref, out_ref):
    own = keep_ref[...] + got_ref[...]
    place = lax.broadcasted_iota(jnp.int32, (SLOTS, ROWS), 0)
    total = None
    for m in range(MICRO):
        cols = slice(m * ROWS, (m + 1) * ROWS)
        hit = (place == slot_ref[0:1, cols]) | (place == slot_ref[1:2, cols])
        part = nt(jnp.where(hit, 1.0, 0.0).astype(BF16), own[cols, :])
        total = part if total is None else total + part
    out_ref[...] = total.astype(BF16)


def owner_kernel(rows_ref, arrived_ref, quot_ref, rem_ref):
    row = lax.broadcasted_iota(jnp.int32, (2 * QROW_DEV, SLOTS), 0)
    picks = jnp.where(row == rows_ref[...], 1.0, 0.0).astype(BF16)
    total = nn(picks, arrived_ref[...])
    quot_ref[...] = total[:QROW_DEV]
    rem_ref[...] = total[QROW_DEV:]


def shards(
    top_grad, layer_inputs, saved_pre, weight_in, weight_out, gain_in, gain_mid, lengths, quot_ids, rem_ids
):
    gain_t, *saved = forward(
        lengths.reshape(MICRO, 4), saved_pre[0], layer_inputs[0], top_grad, gain_mid, gain_in
    )
    *weights, ids = gather_weights(weight_in, weight_out, quot_ids, rem_ids)
    kept = [(*saved[4 * m:4 * m + 3], gain_t) for m in range(MICRO)]
    carried = [saved[4 * m + 3] for m in range(MICRO)]
    before, first = None, None
    for hop in range(SECTIONS):
        section = SECTIONS - 1 - hop
        for micro in range(MICRO):
            last = section == 0 and micro == 1
            extra = () if before is None else (before,)
            if section == 0 and micro == 0:
                extra = extra + (slots, rows)
            out = layer_step(
                section, carried[micro], first if last else None, kept[micro], weights, extra
            )
            if last:
                pieces = out
            elif section == 0:
                before = first = out
            else:
                before = out
                carried[micro] = lax.ppermute(out, "section", [(section, section - 1)])
        if section == 1:
            slots = pl.pallas_call(
                slots_kernel,
                in_specs=[VMEM, VMEM, HBM],
                out_specs=VMEM,
                out_shape=jax.ShapeDtypeStruct((2, MICRO * ROWS), jnp.int32),
                compiler_params=params(16),
                cost_estimate=cost(10**7, 8192),
                name="find_slots",
            )(quot_ids, rem_ids, before)
            rows = pl.pallas_call(
                rows_kernel,
                in_specs=[VMEM, HBM],
                out_specs=VMEM,
                out_shape=jax.ShapeDtypeStruct((1, SLOTS), jnp.int32),
                scratch_shapes=[pltpu.VMEM((SHARDS, 16, ROWS), F32)],
                compiler_params=params(32),
                cost_estimate=cost(3 * 10**7, MIB),
                name="find_rows",
            )(ids, before)

    got = [lax.ppermute(pieces[y], "section", [(0, 2 * y)]) for y in (2, 1, 3)]
    keep, give = pl.pallas_call(
        relay_kernel,
        in_specs=[VMEM] * 4,
        out_specs=[VMEM, VMEM],
        out_shape=[jax.ShapeDtypeStruct((2 * ROWS, ROWS), BF16)] * 2,
        compiler_params=params(16),
        cost_estimate=cost(10**6, MIB),
        name="relay",
    )(pieces[0], *got)
    give = lax.ppermute(give, "section", [(s, s + 1) for s in range(0, SECTIONS, 2)])
    send = pl.pallas_call(
        send_kernel,
        in_specs=[VMEM] * 3,
        out_specs=VMEM,
        out_shape=jax.ShapeDtypeStruct((SLOTS, 128), BF16),
        compiler_params=params(32),
        cost_estimate=cost(7 * 10**7, MIB),
        name="fill_slots",
    )(slots, keep, give)
    arrived = lax.all_to_all(
        send.reshape(SHARDS, 2 * CAP, 128), "shard", split_axis=0, concat_axis=0, tiled=True
    )
    return pl.pallas_call(
        owner_kernel,
        in_specs=[VMEM, VMEM],
        out_specs=[VMEM, VMEM],
        out_shape=[jax.ShapeDtypeStruct((QROW_DEV, 128), F32)] * 2,
        compiler_params=params(32),
        cost_estimate=cost(4 * 10**7, MIB),
        name="owner_sums",
    )(rows, arrived.reshape(SLOTS, 128))


def solution(mesh):
    placed = (
        P(None, "shard", None),
        P("section", None, "shard", None),
        P("section", None, "shard", None),
        P("section", "shard", None),
        P("section", "shard", None),
        P("section", None),
        P("section", None),
        P(None, "shard", None),
        P(None, "shard"),
        P(None, "shard"),
    )
    return jax.shard_map(
        shards,
        mesh=mesh,
        in_specs=placed,
        out_specs=(P("shard", "section"), P("shard", "section")),
        check_vma=False,
    )
```

```python
import functools
import math

import jax
import jax.numpy as jnp
from jax import lax
from jax.experimental import pallas as pl
from jax.experimental.pallas import tpu as pltpu
from jax.sharding import PartitionSpec as P

HEADS = 4
HEAD = 128
ATT = 512
ROWS = 128
WIDTH = 1024
SECTIONS = 8
MICRO = 2
SHARDS = 64
X_SIZE = 4
Z_SIZE = 16
QROW_DEV = 64
CAP = 8
SLOTS = SHARDS * 2 * CAP
EPSILON = 1e-05
BF16 = jnp.bfloat16
F32 = jnp.float32
MIB = 1024 * 1024
VMEM = pl.BlockSpec(memory_space=pltpu.VMEM)
HBM = pl.BlockSpec(memory_space=pl.ANY)

UGR, XHAT, EU, SV, SQ, SK, KT, QT, VN, AN, PT = range(11)
SAVED = 11


def nt(a, b):
    return lax.dot_general(a, b, (((1,), (1,)), ((), ())), preferred_element_type=F32)


def nn(a, b):
    return jnp.dot(a, b, preferred_element_type=F32)


def params(mib):
    return pltpu.CompilerParams(vmem_limit_bytes=mib * MIB)


def cost(flops, size):
    return pl.CostEstimate(flops=flops, bytes_accessed=size, transcendentals=0)


def segment_grid(len_ref, micro, dim):
    place = lax.broadcasted_iota(jnp.int32, (ROWS, ROWS), dim)
    end = jnp.int32(0)
    seg = jnp.zeros((ROWS, ROWS), jnp.int32)
    for k in range(4):
        end = end + len_ref[micro, k]
        seg = seg + (place >= end).astype(jnp.int32)
    return place, seg


def forward_kernel(len_ref, pre_hbm, x_hbm, top_hbm, gain_mid_ref, gain_in_ref, gain_t_ref, *refs):
    out_refs, (pre_ref, x_ref, top_ref, sems) = refs[:4 * MICRO], refs[4 * MICRO:]
    copies = []
    for k, (src, dst) in enumerate(((pre_hbm, pre_ref), (x_hbm, x_ref), (top_hbm, top_ref))):
        for micro in range(MICRO):
            copies.append(pltpu.make_async_copy(src.at[micro], dst.at[micro], sems.at[k, micro]))
            copies[-1].start()
    gain_t_ref[...] = jnp.broadcast_to(gain_in_ref[...], (ROWS, WIDTH)).T
    for one in copies:
        one.wait()
    for micro in range(MICRO):
        saved_ref, xh_ref, rstd_ref, top_t_ref = out_refs[4 * micro:4 * micro + 4]
        forward_part(len_ref, micro, pre_ref, x_ref, top_ref, gain_mid_ref[...],
                     saved_ref, xh_ref, rstd_ref, top_t_ref)


def forward_part(len_ref, micro, pre_ref, x_ref, top_ref, gain, saved_ref, xh_ref, rstd_ref, top_t_ref):
    def act(block):
        pre = pre_ref[micro, :, block * ATT:(block + 1) * ATT].astype(F32)
        sig = jax.nn.sigmoid(pre)
        return pre * sig, sig * (1.0 + pre * (1.0 - sig))

    row, seg_row = segment_grid(len_ref, micro, 0)
    col, seg_col = segment_grid(len_ref, micro, 1)
    same = seg_row == seg_col
    allowed = same & (col <= row)
    allowed_t = same & (row <= col)
    val, dval = act(1)
    que, dque = act(2)
    key, dkey = act(3)
    saved_ref[SV] = dval.T.astype(BF16)
    saved_ref[SQ] = dque.T.astype(BF16)
    saved_ref[SK] = dkey.T.astype(BF16)
    saved_ref[KT] = key.T.astype(BF16)
    saved_ref[QT] = que.T.astype(BF16)
    val, que, key = val.astype(BF16), que.astype(BF16), key.astype(BF16)
    scale = 1.0 / math.sqrt(HEAD)
    mixture = []
    for h in range(HEADS):
        cols = slice(h * HEAD, (h + 1) * HEAD)
        scores = nt(que[:, cols], key[:, cols]) * scale
        soft = jnp.where(allowed, scores * jax.nn.sigmoid(scores), 0.0).astype(BF16)
        scores = nt(key[:, cols], que[:, cols]) * scale
        sig = jax.nn.sigmoid(scores)
        slope = jnp.where(allowed_t, sig * (1.0 + scores * (1.0 - sig)) * scale, 0.0)
        saved_ref[VN, cols, :] = val[:, cols]
        saved_ref[AN, cols, :] = soft
        saved_ref[PT, cols, :] = slope.astype(BF16)
        mixture.append(nn(soft, val[:, cols]))
    mixture = jnp.concatenate(mixture, axis=1)
    centred = mixture - jnp.mean(mixture, axis=1, keepdims=True)
    rstd = lax.rsqrt(jnp.mean(centred * centred, axis=1, keepdims=True) + EPSILON)
    xhat = centred * rstd
    gate, dgate = act(0)
    saved_ref[UGR] = (gate * gain * rstd).T.astype(BF16)
    saved_ref[XHAT] = xhat.T.astype(BF16)
    saved_ref[EU] = (xhat * gain * dgate).T.astype(BF16)
    x = x_ref[micro].astype(F32).T
    x = x - jnp.mean(x, axis=0, keepdims=True)
    rstd = lax.rsqrt(jnp.mean(x * x, axis=0, keepdims=True) + EPSILON)
    xh_ref[...] = (x * rstd).astype(BF16)
    rstd_ref[...] = jnp.broadcast_to(rstd, (8, ROWS))
    top_t_ref[...] = top_ref[micro].astype(F32).T.astype(BF16)


def forward(lengths, pre, x, top, gain_mid, gain_in):
    smem = pl.BlockSpec(memory_space=pltpu.SMEM)
    tall = jax.ShapeDtypeStruct((WIDTH, ROWS), BF16)
    each = [
        jax.ShapeDtypeStruct((SAVED, ATT, ROWS), BF16),
        tall,
        jax.ShapeDtypeStruct((8, ROWS), F32),
        tall,
    ]
    return pl.pallas_call(
        forward_kernel,
        in_specs=[smem] + [pl.BlockSpec(memory_space=pltpu.HBM)] * 3 + [VMEM] * 2,
        out_specs=[VMEM] * 9,
        out_shape=[jax.ShapeDtypeStruct((WIDTH, ROWS), F32)] + each * MICRO,
        scratch_shapes=[
            pltpu.VMEM((MICRO, ROWS, 4 * ATT), BF16),
            pltpu.VMEM((MICRO, ROWS, WIDTH), BF16),
            pltpu.VMEM((MICRO, ROWS, WIDTH), BF16),
            pltpu.SemaphoreType.DMA((3, MICRO)),
        ],
        compiler_params=params(32),
        cost_estimate=cost(2 * 10**8, 6 * MIB),
        name="saved_parts",
    )(lengths, pre, x, top, gain_mid, gain_in)


HALVES = 2048
IDS = HALVES + 512
LINE = IDS + ROWS


def join_kernel(w_in_ref, w_out_ref, quot_ref, rem_ref, out_ref):
    out_ref[:, :HALVES] = w_in_ref[0]
    wide = w_out_ref[0].astype(F32)
    halves = jnp.concatenate([wide[:, :512], wide[:, 512:]], axis=0)
    out_ref[:, HALVES:IDS] = halves.astype(BF16)
    ids = jnp.concatenate([quot_ref[...], rem_ref[...]], axis=0)
    owner = lax.shift_right_logical(ids, 6)
    local = ids - owner * QROW_DEV
    blank = jnp.zeros((8, ROWS), F32)
    coded = jnp.concatenate([owner.astype(F32), local.astype(F32), blank], axis=0)
    out_ref[:, IDS:] = coded.astype(BF16)


def pair_kernel(own_ref, next_ref, out_ref):
    rows = own_ref.shape[0]
    out_ref[:rows, :] = own_ref[...]
    out_ref[rows:, :] = next_ref[...]


def pair(own, other):
    rows, width = own.shape
    return pl.pallas_call(
        pair_kernel,
        in_specs=[VMEM, VMEM],
        out_specs=VMEM,
        out_shape=jax.ShapeDtypeStruct((2 * rows, width), BF16),
        compiler_params=params(16),
        cost_estimate=cost(1000, 8 * rows * width),
        name="pair_weights",
    )(own, other)


def along(value, dx, dz):
    pairs = []
    for x in range(X_SIZE):
        for z in range(Z_SIZE):
            to = (x + dx) % X_SIZE * Z_SIZE + (z + dz) % Z_SIZE
            pairs.append((x * Z_SIZE + z, to))
    return lax.ppermute(value, "shard", pairs)


def swapped(value, bit):
    pairs = []
    for x in range(X_SIZE):
        pairs += [(x * Z_SIZE + z, (x ^ bit) * Z_SIZE + z) for z in range(Z_SIZE)]
    return lax.ppermute(value, "shard", pairs)


def gather_weights(weight_in, weight_out, quot_ids, rem_ids):
    own = pl.pallas_call(
        join_kernel,
        in_specs=[VMEM] * 4,
        out_specs=VMEM,
        out_shape=jax.ShapeDtypeStruct((16, LINE), BF16),
        compiler_params=params(16),
        cost_estimate=cost(1000, 160 * 1024),
        name="join_weights",
    )(weight_in, weight_out, quot_ids, rem_ids)
    block = pair(own, along(own, -1, 0))
    block = pair(block, along(block, -2, 0))
    blocks, offsets = [block], [0]
    up = down = block
    half = Z_SIZE // 2
    for hop in range(1, half + 1):
        up = along(up, 0, 1)
        blocks.append(up)
        offsets.append(-hop)
        if hop < half:
            down = along(down, 0, -1)
            blocks.append(down)
            offsets.append(hop)
    return pl.pallas_call(
        functools.partial(place_kernel, tuple(offsets)),
        in_specs=[VMEM] * Z_SIZE,
        out_specs=[VMEM] * 3,
        out_shape=[
            jax.ShapeDtypeStruct((Z_SIZE, 64, 2048), BF16),
            jax.ShapeDtypeStruct((Z_SIZE, 16, 2048), BF16),
            jax.ShapeDtypeStruct((Z_SIZE, X_SIZE, 16, ROWS), BF16),
        ],
        scratch_shapes=[pltpu.VMEM((Z_SIZE, 32, 1024), F32)],
        compiler_params=params(32),
        cost_estimate=cost(1000, 10 * MIB),
        name="place_weights",
    )(*blocks)


def place_kernel(offsets, *refs):
    blocks, (w_in_ref, w_out_ref, ids_ref, wide) = refs[:Z_SIZE], refs[Z_SIZE:]
    here_x = lax.axis_index("shard") // Z_SIZE
    here_z = lax.axis_index("shard") % Z_SIZE
    for block, offset in zip(blocks, offsets):
        z = (here_z + Z_SIZE + offset) % Z_SIZE
        for step in range(X_SIZE):
            x = (here_x + step) % X_SIZE
            rows = slice(step * 16, (step + 1) * 16)
            w_in_ref[z, pl.ds(pl.multiple_of(x * 16, 16), 16), :] = block[rows, :HALVES]
            ids_ref[z, x] = block[rows, IDS:]
            halves = block[rows, HALVES:IDS].astype(F32)
            at = pl.ds(pl.multiple_of(x * 8, 8), 8)
            wide[z, at, 0:512] = halves[0:8]
            wide[z, at, 512:1024] = halves[8:16]
    for z in range(Z_SIZE):
        w_out_ref[z, :, 0:1024] = wide[z, 0:16, :].astype(BF16)
        w_out_ref[z, :, 1024:2048] = wide[z, 16:32, :].astype(BF16)


def step_kernel(at_section, last, n_extra, *refs):
    refs = list(refs)
    g_ref = refs.pop(0)
    first_ref = refs.pop(0) if last else None
    saved, xh, rstd, gain, w_in, w_out = refs[:6]
    outs, gp = refs[6 + n_extra:-1], refs[-1]

    @pl.when(lax.axis_index("section") == at_section)
    def _():
        grad = g_ref[...]
        grad_mid = []
        for half in range(2):
            weight = w_out[:, :, half * 1024:(half + 1) * 1024].reshape(256, 1024)
            both = nn(weight, grad).reshape(Z_SIZE, 2, 8, ROWS)
            grad_mid += [both[:, 0].reshape(HEAD, ROWS), both[:, 1].reshape(HEAD, ROWS)]

        def part(name, h):
            return saved[name, h * HEAD:(h + 1) * HEAD, :]

        terms = [grad_mid[h] * part(UGR, h).astype(F32) for h in range(HEADS)]
        xhats = [part(XHAT, h).astype(F32) for h in range(HEADS)]
        mean_1 = sum(terms[1:], terms[0])
        mean_2 = terms[0] * xhats[0]
        for h in range(1, HEADS):
            mean_2 = mean_2 + terms[h] * xhats[h]
        mean_1 = jnp.sum(mean_1, axis=0, keepdims=True) * (1.0 / ATT)
        mean_2 = jnp.sum(mean_2, axis=0, keepdims=True) * (1.0 / ATT)
        for h in range(HEADS):
            def put(block, value):
                start = block * ATT + h * HEAD
                gp[start:start + HEAD, :] = value.astype(BF16)

            put(0, grad_mid[h] * part(EU, h).astype(F32))
            d_o = (terms[h] - mean_1 - xhats[h] * mean_2).astype(BF16)
            d_s = (nn(part(VN, h), d_o) * part(PT, h).astype(F32)).astype(BF16)
            put(1, nn(d_o, part(AN, h)) * part(SV, h).astype(F32))
            put(2, nn(part(KT, h), d_s) * part(SQ, h).astype(F32))
            put(3, nt(part(QT, h), d_s) * part(SK, h).astype(F32))
        product = nn(w_in[...].reshape(WIDTH, 4 * ATT), gp[...])
        product = product.reshape(Z_SIZE, X_SIZE, 16, ROWS)
        d_xh, x_hat = [], []
        for x in range(X_SIZE):
            rows = slice(x * 256, (x + 1) * 256)
            d_xh.append(product[:, x].reshape(256, ROWS) * gain[rows, :])
            x_hat.append(xh[rows, :].astype(F32))
        mean_1 = sum(d_xh[1:], d_xh[0])
        mean_2 = d_xh[0] * x_hat[0]
        for x in range(1, X_SIZE):
            mean_2 = mean_2 + d_xh[x] * x_hat[x]
        mean_1 = jnp.sum(mean_1, axis=0, keepdims=True) * (1.0 / WIDTH)
        mean_2 = jnp.sum(mean_2, axis=0, keepdims=True) * (1.0 / WIDTH)
        scale = rstd[0:1, :]
        for x in range(X_SIZE):
            rows = slice(x * 256, (x + 1) * 256)
            d_x = (d_xh[x] - mean_1 - x_hat[x] * mean_2) * scale
            result = (grad[rows, :].astype(F32) + d_x).astype(BF16)
            if last:
                outs[x][ROWS:2 * ROWS, :] = result[0:128]
                outs[x][3 * ROWS:, :] = result[128:256]
            else:
                outs[0][rows, :] = result
        if last:
            for x in range(X_SIZE):
                outs[x][0:ROWS, :] = first_ref[x * 256:x * 256 + 128, :]
                outs[x][2 * ROWS:3 * ROWS, :] = first_ref[x * 256 + 128:(x + 1) * 256, :]


def layer_step(at_section, grad, first, kept, weights, extra):
    last = first is not None
    operands = [grad, first] if last else [grad]
    operands += [*kept, *weights]
    if last:
        out_shape = [jax.ShapeDtypeStruct((4 * ROWS, ROWS), BF16)] * (SECTIONS // 2)
    else:
        out_shape = [jax.ShapeDtypeStruct((WIDTH, ROWS), BF16)]
    out = pl.pallas_call(
        functools.partial(step_kernel, at_section, last, len(extra)),
        in_specs=[VMEM] * len(operands) + [HBM] * len(extra),
        out_specs=[VMEM] * len(out_shape),
        out_shape=out_shape,
        scratch_shapes=[pltpu.VMEM((4 * ATT, ROWS), BF16)],
        compiler_params=params(32),
        cost_estimate=cost(7 * 10**8, 8 * MIB),
        name="layer_step",
    )(*operands, *extra)
    return out if last else out[0]


def earlier_mask():
    tokens = MICRO * ROWS
    before = (
        lax.broadcasted_iota(jnp.int32, (tokens, tokens), 0)
        < lax.broadcasted_iota(jnp.int32, (tokens, tokens), 1)
    )
    return jnp.where(before, 1.0, 0.0).astype(BF16)


def slots_kernel(ids_ref, _, slot_ref):
    here_x = lax.axis_index("shard") // Z_SIZE
    here_z = lax.axis_index("shard") % Z_SIZE
    owners = lax.broadcasted_iota(jnp.int32, (SHARDS, MICRO * ROWS), 0)
    before = earlier_mask()
    for e in range(X_SIZE):
        coded = ids_ref[here_z, jnp.bitwise_xor(here_x, e)].astype(F32)
        for table in range(2):
            row = 2 * table
            owner = jnp.concatenate([coded[row:row + 1, :], coded[row + 1:row + 2, :]], axis=1)
            owner = owner.astype(jnp.int32)
            one_hot = jnp.where(owners == owner, 1.0, 0.0)
            earlier = nn(one_hot.astype(BF16), before)
            rank = jnp.sum(earlier * one_hot, axis=0, keepdims=True).astype(jnp.int32)
            x = lax.shift_right_logical(owner, 4)
            slot = (owner - x * Z_SIZE) * (2 * CAP) + rank + table * CAP
            slot_ref[2 * e + table:2 * e + table + 1, :] = jnp.where(x == here_x, slot, -1)


def rows_kernel(ids_ref, _, rows_ref, wide_ids):
    here = lax.axis_index("shard").astype(F32)
    here_x = lax.axis_index("shard") // Z_SIZE
    before = earlier_mask()
    lane = lax.broadcasted_iota(jnp.int32, (SHARDS, 128), 1)
    total = jnp.zeros((SHARDS, 128), F32)
    wide_ids[...] = ids_ref[...].reshape(SHARDS, 16, ROWS).astype(F32)

    def both(row):
        return jnp.concatenate([wide_ids[:, row, :], wide_ids[:, row + 1, :]], axis=1)

    for table in range(2):
        mine = both(2 * table) == here
        rank = nn(jnp.where(mine, 1.0, 0.0).astype(BF16), before)
        local = both(2 * MICRO + 2 * table) + (1.0 + table * QROW_DEV)
        for k in range(CAP):
            value = jnp.where(mine & (rank == float(k)), local, 0.0)
            value = jnp.sum(value, axis=1, keepdims=True)
            total = total + jnp.where(lane == table * CAP + k, value, 0.0)
    slot = lax.broadcasted_iota(jnp.int32, (128, SLOTS), 1)
    spread = jnp.where(slot % (2 * CAP) == lax.broadcasted_iota(jnp.int32, (128, SLOTS), 0), 1.0, 0.0)
    wide = nn(total.astype(BF16), spread.astype(BF16))
    slot = lax.broadcasted_iota(jnp.int32, (SHARDS, SLOTS), 1)
    place = lax.broadcasted_iota(jnp.int32, (SHARDS, SLOTS), 0)
    x = jnp.bitwise_xor(slot // (2 * CAP) % X_SIZE, here_x)
    own = place == slot // (2 * CAP * X_SIZE) * X_SIZE + x
    wide = jnp.sum(jnp.where(own, wide, 0.0), axis=0, keepdims=True)
    rows_ref[...] = wide.astype(jnp.int32) - 1


def relay_kernel(own_ref, *refs):
    got, (keep_ref, give_ref) = refs[:-2], refs[-2:]
    total = got[0][...]
    for one in got[1:]:
        total = total + one[...]
    total = jnp.where(lax.axis_index("section") == 0, own_ref[...], total)
    keep_ref[...] = total[:2 * ROWS]
    give_ref[...] = total[2 * ROWS:]


def add_kernel(keep_ref, got_ref, out_ref):
    out_ref[...] = keep_ref[...] + got_ref[...]


def send_kernel(slot_ref, near_ref, far_ref, out_ref):
    place = lax.broadcasted_iota(jnp.int32, (Z_SIZE * 2 * CAP, ROWS), 0)
    for e in range(X_SIZE):
        ref = far_ref if e >= 2 else near_ref
        total = None
        for m in range(MICRO):
            cols = slice(m * ROWS, (m + 1) * ROWS)
            hit = (place == slot_ref[2 * e:2 * e + 1, cols]) | (place == slot_ref[2 * e + 1:2 * e + 2, cols])
            start = (e % 2 * MICRO + m) * ROWS
            part = nt(jnp.where(hit, 1.0, 0.0).astype(BF16), ref[start:start + ROWS, :])
            total = part if total is None else total + part
        total = total.astype(BF16).reshape(Z_SIZE, 2 * CAP, 128)
        out_ref[:, e * 2 * CAP:(e + 1) * 2 * CAP, :] = total


def owner_kernel(rows_ref, arrived_ref, quot_ref, rem_ref):
    row = lax.broadcasted_iota(jnp.int32, (2 * QROW_DEV, SLOTS), 0)
    picks = jnp.where(row == rows_ref[...], 1.0, 0.0).astype(BF16)
    total = nn(picks, arrived_ref[...])
    quot_ref[...] = total[:QROW_DEV]
    rem_ref[...] = total[QROW_DEV:]


def shards(
    top_grad, layer_inputs, saved_pre, weight_in, weight_out, gain_in, gain_mid, lengths, quot_ids, rem_ids
):
    gain_t, *saved = forward(
        lengths.reshape(MICRO, 4), saved_pre[0], layer_inputs[0], top_grad, gain_mid, gain_in
    )
    *weights, ids = gather_weights(weight_in, weight_out, quot_ids, rem_ids)
    kept = [(*saved[4 * m:4 * m + 3], gain_t) for m in range(MICRO)]
    carried = [saved[4 * m + 3] for m in range(MICRO)]
    before, first = None, None
    for hop in range(SECTIONS):
        section = SECTIONS - 1 - hop
        for micro in range(MICRO):
            last = section == 0 and micro == 1
            extra = () if before is None else (before,)
            if section == 0 and micro == 0:
                extra = extra + (slots, rows)
            out = layer_step(
                section, carried[micro], first if last else None, kept[micro], weights, extra
            )
            if last:
                pieces = out
            elif section == 0:
                before = first = out
            else:
                before = out
                carried[micro] = lax.ppermute(out, "section", [(section, section - 1)])
        if section == 1:
            slots = pl.pallas_call(
                slots_kernel,
                in_specs=[VMEM, HBM],
                out_specs=VMEM,
                out_shape=jax.ShapeDtypeStruct((2 * X_SIZE, MICRO * ROWS), jnp.int32),
                compiler_params=params(16),
                cost_estimate=cost(10**7, 8192),
                name="find_slots",
            )(ids, before)
            rows = pl.pallas_call(
                rows_kernel,
                in_specs=[VMEM, HBM],
                out_specs=VMEM,
                out_shape=jax.ShapeDtypeStruct((1, SLOTS), jnp.int32),
                scratch_shapes=[pltpu.VMEM((SHARDS, 16, ROWS), F32)],
                compiler_params=params(32),
                cost_estimate=cost(3 * 10**7, MIB),
                name="find_rows",
            )(ids, before)

    got = [lax.ppermute(pieces[y], "section", [(0, 2 * y)]) for y in (2, 1, 3)]
    keep, give = pl.pallas_call(
        relay_kernel,
        in_specs=[VMEM] * 4,
        out_specs=[VMEM, VMEM],
        out_shape=[jax.ShapeDtypeStruct((2 * ROWS, ROWS), BF16)] * 2,
        compiler_params=params(16),
        cost_estimate=cost(10**6, MIB),
        name="relay",
    )(pieces[0], *got)
    give = lax.ppermute(give, "section", [(s, s + 1) for s in range(0, SECTIONS, 2)])
    own = pl.pallas_call(
        add_kernel,
        in_specs=[VMEM, VMEM],
        out_specs=VMEM,
        out_shape=jax.ShapeDtypeStruct((2 * ROWS, ROWS), BF16),
        compiler_params=params(16),
        cost_estimate=cost(10**5, 3 * 2**16),
        name="own_columns",
    )(keep, give)
    near = pair(own, swapped(own, 1))
    send = pl.pallas_call(
        send_kernel,
        in_specs=[VMEM] * 3,
        out_specs=VMEM,
        out_shape=jax.ShapeDtypeStruct((Z_SIZE, X_SIZE * 2 * CAP, 128), BF16),
        compiler_params=params(32),
        cost_estimate=cost(7 * 10**7, MIB),
        name="fill_slots",
    )(slots, near, swapped(near, 2))
    arrived = lax.all_to_all(
        send, "shard", split_axis=0, concat_axis=0, tiled=True,
        axis_index_groups=[[x * Z_SIZE + z for z in range(Z_SIZE)] for x in range(X_SIZE)],
    )
    return pl.pallas_call(
        owner_kernel,
        in_specs=[VMEM, VMEM],
        out_specs=[VMEM, VMEM],
        out_shape=[jax.ShapeDtypeStruct((QROW_DEV, 128), F32)] * 2,
        compiler_params=params(32),
        cost_estimate=cost(4 * 10**7, MIB),
        name="owner_sums",
    )(rows, arrived.reshape(SLOTS, 128))


def solution(mesh):
    placed = (
        P(None, "shard", None),
        P("section", None, "shard", None),
        P("section", None, "shard", None),
        P("section", "shard", None),
        P("section", "shard", None),
        P("section", None),
        P("section", None),
        P(None, "shard", None),
        P(None, "shard"),
        P(None, "shard"),
    )
    return jax.shard_map(
        shards,
        mesh=mesh,
        in_specs=placed,
        out_specs=(P("shard", "section"), P("shard", "section")),
        check_vma=False,
    )
```

```python
import functools
import math

import jax
import jax.numpy as jnp
from jax import lax
from jax.experimental import pallas as pl
from jax.experimental.pallas import tpu as pltpu
from jax.sharding import PartitionSpec as P

HEADS = 4
HEAD = 128
ATT = 512
ROWS = 128
WIDTH = 1024
SECTIONS = 8
MICRO = 2
SHARDS = 64
X_SIZE = 4
Z_SIZE = 16
QROW_DEV = 64
CAP = 8
SLOTS = SHARDS * 2 * CAP
EPSILON = 1e-05
BF16 = jnp.bfloat16
F32 = jnp.float32
MIB = 1024 * 1024
VMEM = pl.BlockSpec(memory_space=pltpu.VMEM)
HBM = pl.BlockSpec(memory_space=pl.ANY)

UGR, XHAT, EU, SV, SQ, SK, KT, QT, VN, AN, PT = range(11)
SAVED = 11


def nt(a, b):
    return lax.dot_general(a, b, (((1,), (1,)), ((), ())), preferred_element_type=F32)


def nn(a, b):
    return jnp.dot(a, b, preferred_element_type=F32)


def params(mib):
    return pltpu.CompilerParams(vmem_limit_bytes=mib * MIB)


def cost(flops, size):
    return pl.CostEstimate(flops=flops, bytes_accessed=size, transcendentals=0)


def segment_grid(len_ref, micro, dim):
    place = lax.broadcasted_iota(jnp.int32, (ROWS, ROWS), dim)
    end = jnp.int32(0)
    seg = jnp.zeros((ROWS, ROWS), jnp.int32)
    for k in range(4):
        end = end + len_ref[micro, k]
        seg = seg + (place >= end).astype(jnp.int32)
    return place, seg


def forward_kernel(len_ref, pre_hbm, x_hbm, top_hbm, gain_mid_ref, gain_in_ref, gain_t_ref, *refs):
    out_refs, (pre_ref, x_ref, top_ref, sems) = refs[:4 * MICRO], refs[4 * MICRO:]
    copies = []
    for k, (src, dst) in enumerate(((pre_hbm, pre_ref), (x_hbm, x_ref), (top_hbm, top_ref))):
        for micro in range(MICRO):
            copies.append(pltpu.make_async_copy(src.at[micro], dst.at[micro], sems.at[k, micro]))
            copies[-1].start()
    gain_t_ref[...] = jnp.broadcast_to(gain_in_ref[...], (ROWS, WIDTH)).T
    for one in copies:
        one.wait()
    for micro in range(MICRO):
        saved_ref, xh_ref, rstd_ref, top_t_ref = out_refs[4 * micro:4 * micro + 4]
        forward_part(len_ref, micro, pre_ref, x_ref, top_ref, gain_mid_ref[...],
                     saved_ref, xh_ref, rstd_ref, top_t_ref)


def forward_part(len_ref, micro, pre_ref, x_ref, top_ref, gain, saved_ref, xh_ref, rstd_ref, top_t_ref):
    def act(block):
        pre = pre_ref[micro, :, block * ATT:(block + 1) * ATT].astype(F32)
        sig = jax.nn.sigmoid(pre)
        return pre * sig, sig * (1.0 + pre * (1.0 - sig))

    row, seg_row = segment_grid(len_ref, micro, 0)
    col, seg_col = segment_grid(len_ref, micro, 1)
    same = seg_row == seg_col
    allowed = same & (col <= row)
    allowed_t = same & (row <= col)
    val, dval = act(1)
    que, dque = act(2)
    key, dkey = act(3)
    saved_ref[SV] = dval.T.astype(BF16)
    saved_ref[SQ] = dque.T.astype(BF16)
    saved_ref[SK] = dkey.T.astype(BF16)
    saved_ref[KT] = key.T.astype(BF16)
    saved_ref[QT] = que.T.astype(BF16)
    val, que, key = val.astype(BF16), que.astype(BF16), key.astype(BF16)
    scale = 1.0 / math.sqrt(HEAD)
    mixture = []
    for h in range(HEADS):
        cols = slice(h * HEAD, (h + 1) * HEAD)
        scores = nt(que[:, cols], key[:, cols]) * scale
        soft = jnp.where(allowed, scores * jax.nn.sigmoid(scores), 0.0).astype(BF16)
        scores = nt(key[:, cols], que[:, cols]) * scale
        sig = jax.nn.sigmoid(scores)
        slope = jnp.where(allowed_t, sig * (1.0 + scores * (1.0 - sig)) * scale, 0.0)
        saved_ref[VN, cols, :] = val[:, cols]
        saved_ref[AN, cols, :] = soft
        saved_ref[PT, cols, :] = slope.astype(BF16)
        mixture.append(nn(soft, val[:, cols]))
    mixture = jnp.concatenate(mixture, axis=1)
    centred = mixture - jnp.mean(mixture, axis=1, keepdims=True)
    rstd = lax.rsqrt(jnp.mean(centred * centred, axis=1, keepdims=True) + EPSILON)
    xhat = centred * rstd
    gate, dgate = act(0)
    saved_ref[UGR] = (gate * gain * rstd).T.astype(BF16)
    saved_ref[XHAT] = xhat.T.astype(BF16)
    saved_ref[EU] = (xhat * gain * dgate).T.astype(BF16)
    x = x_ref[micro].astype(F32).T
    x = x - jnp.mean(x, axis=0, keepdims=True)
    rstd = lax.rsqrt(jnp.mean(x * x, axis=0, keepdims=True) + EPSILON)
    xh_ref[...] = (x * rstd).astype(BF16)
    rstd_ref[...] = jnp.broadcast_to(rstd, (8, ROWS))
    top_t_ref[...] = top_ref[micro].astype(F32).T.astype(BF16)


def forward(lengths, pre, x, top, gain_mid, gain_in):
    smem = pl.BlockSpec(memory_space=pltpu.SMEM)
    tall = jax.ShapeDtypeStruct((WIDTH, ROWS), BF16)
    each = [
        jax.ShapeDtypeStruct((SAVED, ATT, ROWS), BF16),
        tall,
        jax.ShapeDtypeStruct((8, ROWS), F32),
        tall,
    ]
    return pl.pallas_call(
        forward_kernel,
        in_specs=[smem] + [pl.BlockSpec(memory_space=pltpu.HBM)] * 3 + [VMEM] * 2,
        out_specs=[VMEM] * 9,
        out_shape=[jax.ShapeDtypeStruct((WIDTH, ROWS), F32)] + each * MICRO,
        scratch_shapes=[
            pltpu.VMEM((MICRO, ROWS, 4 * ATT), BF16),
            pltpu.VMEM((MICRO, ROWS, WIDTH), BF16),
            pltpu.VMEM((MICRO, ROWS, WIDTH), BF16),
            pltpu.SemaphoreType.DMA((3, MICRO)),
        ],
        compiler_params=params(32),
        cost_estimate=cost(2 * 10**8, 6 * MIB),
        name="saved_parts",
    )(lengths, pre, x, top, gain_mid, gain_in)


HALVES = 2048
IDS = HALVES + 512
LINE = IDS + ROWS


def join_kernel(w_in_ref, w_out_ref, quot_ref, rem_ref, out_ref):
    out_ref[:, :HALVES] = w_in_ref[0]
    wide = w_out_ref[0].astype(F32)
    halves = jnp.concatenate([wide[:, :512], wide[:, 512:]], axis=0)
    out_ref[:, HALVES:IDS] = halves.astype(BF16)
    ids = jnp.concatenate([quot_ref[...], rem_ref[...]], axis=0)
    owner = lax.shift_right_logical(ids, 6)
    local = ids - owner * QROW_DEV
    blank = jnp.zeros((8, ROWS), F32)
    coded = jnp.concatenate([owner.astype(F32), local.astype(F32), blank], axis=0)
    out_ref[:, IDS:] = coded.astype(BF16)


def pair_kernel(own_ref, next_ref, out_ref):
    rows = own_ref.shape[0]
    out_ref[:rows, :] = own_ref[...]
    out_ref[rows:, :] = next_ref[...]


def pair(own, other):
    return pl.pallas_call(
        pair_kernel,
        in_specs=[VMEM, VMEM],
        out_specs=VMEM,
        out_shape=jax.ShapeDtypeStruct((2 * own.shape[0], LINE), BF16),
        compiler_params=params(16),
        cost_estimate=cost(1000, 4 * own.shape[0] * LINE * 2),
        name="pair_weights",
    )(own, other)


def along(value, dx, dz):
    pairs = []
    for x in range(X_SIZE):
        for z in range(Z_SIZE):
            to = (x + dx) % X_SIZE * Z_SIZE + (z + dz) % Z_SIZE
            pairs.append((x * Z_SIZE + z, to))
    return lax.ppermute(value, "shard", pairs)


def partner(x, side):
    return (x + 1) % X_SIZE if x % 2 == side else (x - 1) % X_SIZE


def across(value, side):
    pairs = []
    for x in range(X_SIZE):
        pairs += [(x * Z_SIZE + z, partner(x, side) * Z_SIZE + z) for z in range(Z_SIZE)]
    return lax.ppermute(value, "shard", pairs)


def pick_kernel(side, n_blocks, gated, n_after, *refs):
    outs = refs[n_blocks + gated + n_after:]
    if gated:
        outs[1][...] = refs[n_blocks][...]
    here_x = lax.axis_index("shard") // Z_SIZE
    start = pl.multiple_of((here_x + side) % 2 * 16, 16)
    for k, ref in enumerate(refs[:n_blocks]):
        outs[0][k * 16:(k + 1) * 16, :] = ref[pl.ds(start, 16), :]


def pick(side, blocks, gate=None, after=()):
    gates = [] if gate is None else [gate]
    shapes = [jax.ShapeDtypeStruct((16 * len(blocks), LINE), BF16)]
    shapes += [jax.ShapeDtypeStruct((32, LINE), BF16)] * len(gates)
    return pl.pallas_call(
        functools.partial(pick_kernel, side, len(blocks), len(gates), len(after)),
        in_specs=[VMEM] * (len(blocks) + len(gates)) + [HBM] * len(after),
        out_specs=[VMEM] * len(shapes),
        out_shape=shapes,
        compiler_params=params(16),
        cost_estimate=cost(1000, len(blocks) * 160 * 1024),
        name="pick_shards",
    )(*blocks, *gates, *after)


def gather_weights(weight_in, weight_out, quot_ids, rem_ids):
    own = pl.pallas_call(
        join_kernel,
        in_specs=[VMEM] * 4,
        out_specs=VMEM,
        out_shape=jax.ShapeDtypeStruct((16, LINE), BF16),
        compiler_params=params(16),
        cost_estimate=cost(1000, 160 * 1024),
        name="join_weights",
    )(weight_in, weight_out, quot_ids, rem_ids)
    block = pair(own, along(own, -1, 0))
    up, down = {0: block}, {}
    half = Z_SIZE // 2
    blocks, offsets, sizes, sides = [], [], [], ([], [])

    def batch_of(hops):
        batch = []
        for hop in hops:
            batch.append(up[hop])
            offsets.append(-hop)
            if hop in down:
                batch.append(down[hop])
                offsets.append(hop)
        blocks.extend(batch)
        sizes.append(len(batch))
        return batch

    gates = {4: (0, 1, 2), 7: (3, 4, 5)}
    for hop in range(1, half + 1):
        last = down[hop - 1] if hop > 1 else block
        if hop in gates:
            batch = batch_of(gates[hop])
            first, up[hop - 1] = pick(0, batch, up[hop - 1], sides[0][-1:])
            second, last = pick(1, batch, last, sides[1][-1:])
            down[hop - 1] = last
            sides[0].append(across(first, 0))
            sides[1].append(across(second, 1))
        up[hop] = along(up[hop - 1], 0, 1)
        if hop < half:
            down[hop] = along(last, 0, -1)
    batch = batch_of((6, 7, 8))
    for side in range(2):
        sides[side].append(across(pick(side, batch, None, sides[side][-1:])[0], side))
    return pl.pallas_call(
        functools.partial(place_kernel, tuple(offsets), tuple(sizes)),
        in_specs=[VMEM] * (Z_SIZE + 2 * len(sizes)),
        out_specs=[VMEM] * 3,
        out_shape=[
            jax.ShapeDtypeStruct((Z_SIZE, 64, 2048), BF16),
            jax.ShapeDtypeStruct((Z_SIZE, 16, 2048), BF16),
            jax.ShapeDtypeStruct((Z_SIZE, X_SIZE, 16, ROWS), BF16),
        ],
        scratch_shapes=[pltpu.VMEM((Z_SIZE, 32, 1024), F32)],
        compiler_params=params(32),
        cost_estimate=cost(1000, 10 * MIB),
        name="place_weights",
    )(*blocks, *sides[0], *sides[1])


def place_kernel(offsets, sizes, *refs):
    blocks, refs = refs[:Z_SIZE], refs[Z_SIZE:]
    sides = refs[:len(sizes)], refs[len(sizes):2 * len(sizes)]
    w_in_ref, w_out_ref, ids_ref, wide = refs[2 * len(sizes):]
    here_x = lax.axis_index("shard") // Z_SIZE
    here_z = lax.axis_index("shard") % Z_SIZE
    odd = here_x % 2
    spots = [(batch, k) for batch, size in enumerate(sizes) for k in range(size)]
    for block, offset, (batch, k) in zip(blocks, offsets, spots):
        z = (here_z + Z_SIZE + offset) % Z_SIZE
        some = slice(k * 16, (k + 1) * 16)
        sources = (
            (block, slice(0, 16), 0),
            (block, slice(16, 32), 1),
            (sides[0][batch], some, 2 + odd),
            (sides[1][batch], some, 3 - odd),
        )
        for ref, rows, step in sources:
            x = (here_x + step) % X_SIZE
            w_in_ref[z, pl.ds(pl.multiple_of(x * 16, 16), 16), :] = ref[rows, :HALVES]
            ids_ref[z, x] = ref[rows, IDS:]
            halves = ref[rows, HALVES:IDS].astype(F32)
            at = pl.ds(pl.multiple_of(x * 8, 8), 8)
            wide[z, at, 0:512] = halves[0:8]
            wide[z, at, 512:1024] = halves[8:16]
    for z in range(Z_SIZE):
        w_out_ref[z, :, 0:1024] = wide[z, 0:16, :].astype(BF16)
        w_out_ref[z, :, 1024:2048] = wide[z, 16:32, :].astype(BF16)


def step_kernel(at_section, last, n_extra, *refs):
    refs = list(refs)
    g_ref = refs.pop(0)
    first_ref = refs.pop(0) if last else None
    saved, xh, rstd, gain, w_in, w_out = refs[:6]
    outs, gp = refs[6 + n_extra:-1], refs[-1]

    @pl.when(lax.axis_index("section") == at_section)
    def _():
        grad = g_ref[...]
        grad_mid = []
        for half in range(2):
            weight = w_out[:, :, half * 1024:(half + 1) * 1024].reshape(256, 1024)
            both = nn(weight, grad).reshape(Z_SIZE, 2, 8, ROWS)
            grad_mid += [both[:, 0].reshape(HEAD, ROWS), both[:, 1].reshape(HEAD, ROWS)]

        def part(name, h):
            return saved[name, h * HEAD:(h + 1) * HEAD, :]

        terms = [grad_mid[h] * part(UGR, h).astype(F32) for h in range(HEADS)]
        xhats = [part(XHAT, h).astype(F32) for h in range(HEADS)]
        mean_1 = sum(terms[1:], terms[0])
        mean_2 = terms[0] * xhats[0]
        for h in range(1, HEADS):
            mean_2 = mean_2 + terms[h] * xhats[h]
        mean_1 = jnp.sum(mean_1, axis=0, keepdims=True) * (1.0 / ATT)
        mean_2 = jnp.sum(mean_2, axis=0, keepdims=True) * (1.0 / ATT)
        for h in range(HEADS):
            def put(block, value):
                start = block * ATT + h * HEAD
                gp[start:start + HEAD, :] = value.astype(BF16)

            put(0, grad_mid[h] * part(EU, h).astype(F32))
            d_o = (terms[h] - mean_1 - xhats[h] * mean_2).astype(BF16)
            d_s = (nn(part(VN, h), d_o) * part(PT, h).astype(F32)).astype(BF16)
            put(1, nn(d_o, part(AN, h)) * part(SV, h).astype(F32))
            put(2, nn(part(KT, h), d_s) * part(SQ, h).astype(F32))
            put(3, nt(part(QT, h), d_s) * part(SK, h).astype(F32))
        product = nn(w_in[...].reshape(WIDTH, 4 * ATT), gp[...])
        product = product.reshape(Z_SIZE, X_SIZE, 16, ROWS)
        d_xh, x_hat = [], []
        for x in range(X_SIZE):
            rows = slice(x * 256, (x + 1) * 256)
            d_xh.append(product[:, x].reshape(256, ROWS) * gain[rows, :])
            x_hat.append(xh[rows, :].astype(F32))
        mean_1 = sum(d_xh[1:], d_xh[0])
        mean_2 = d_xh[0] * x_hat[0]
        for x in range(1, X_SIZE):
            mean_2 = mean_2 + d_xh[x] * x_hat[x]
        mean_1 = jnp.sum(mean_1, axis=0, keepdims=True) * (1.0 / WIDTH)
        mean_2 = jnp.sum(mean_2, axis=0, keepdims=True) * (1.0 / WIDTH)
        scale = rstd[0:1, :]
        for x in range(X_SIZE):
            rows = slice(x * 256, (x + 1) * 256)
            d_x = (d_xh[x] - mean_1 - x_hat[x] * mean_2) * scale
            result = (grad[rows, :].astype(F32) + d_x).astype(BF16)
            if last:
                outs[x][ROWS:2 * ROWS, :] = result[0:128]
                outs[x][3 * ROWS:, :] = result[128:256]
            else:
                outs[0][rows, :] = result
        if last:
            for x in range(X_SIZE):
                outs[x][0:ROWS, :] = first_ref[x * 256:x * 256 + 128, :]
                outs[x][2 * ROWS:3 * ROWS, :] = first_ref[x * 256 + 128:(x + 1) * 256, :]


def layer_step(at_section, grad, first, kept, weights, extra):
    last = first is not None
    operands = [grad, first] if last else [grad]
    operands += [*kept, *weights]
    if last:
        out_shape = [jax.ShapeDtypeStruct((4 * ROWS, ROWS), BF16)] * (SECTIONS // 2)
    else:
        out_shape = [jax.ShapeDtypeStruct((WIDTH, ROWS), BF16)]
    out = pl.pallas_call(
        functools.partial(step_kernel, at_section, last, len(extra)),
        in_specs=[VMEM] * len(operands) + [HBM] * len(extra),
        out_specs=[VMEM] * len(out_shape),
        out_shape=out_shape,
        scratch_shapes=[pltpu.VMEM((4 * ATT, ROWS), BF16)],
        compiler_params=params(32),
        cost_estimate=cost(7 * 10**8, 8 * MIB),
        name="layer_step",
    )(*operands, *extra)
    return out if last else out[0]


def earlier_mask():
    tokens = MICRO * ROWS
    before = (
        lax.broadcasted_iota(jnp.int32, (tokens, tokens), 0)
        < lax.broadcasted_iota(jnp.int32, (tokens, tokens), 1)
    )
    return jnp.where(before, 1.0, 0.0).astype(BF16)


def slots_kernel(quot_ref, rem_ref, _, slot_ref):
    owners = lax.broadcasted_iota(jnp.int32, (SHARDS, MICRO * ROWS), 0)
    before = earlier_mask()
    for table, ref in enumerate((quot_ref, rem_ref)):
        ids = jnp.concatenate([ref[0:1, :], ref[1:2, :]], axis=1)
        owner = lax.shift_right_logical(ids, 6)
        one_hot = jnp.where(owners == owner, 1.0, 0.0)
        earlier = nn(one_hot.astype(BF16), before)
        rank = jnp.sum(earlier * one_hot, axis=0, keepdims=True).astype(jnp.int32)
        slot_ref[table:table + 1, :] = owner * (2 * CAP) + rank + table * CAP


def rows_kernel(ids_ref, _, rows_ref, wide_ids):
    here = lax.axis_index("shard").astype(F32)
    before = earlier_mask()
    lane = lax.broadcasted_iota(jnp.int32, (SHARDS, 128), 1)
    total = jnp.zeros((SHARDS, 128), F32)
    wide_ids[...] = ids_ref[...].reshape(SHARDS, 16, ROWS).astype(F32)

    def both(row):
        return jnp.concatenate([wide_ids[:, row, :], wide_ids[:, row + 1, :]], axis=1)

    for table in range(2):
        mine = both(2 * table) == here
        rank = nn(jnp.where(mine, 1.0, 0.0).astype(BF16), before)
        local = both(2 * MICRO + 2 * table) + (1.0 + table * QROW_DEV)
        for k in range(CAP):
            value = jnp.where(mine & (rank == float(k)), local, 0.0)
            value = jnp.sum(value, axis=1, keepdims=True)
            total = total + jnp.where(lane == table * CAP + k, value, 0.0)
    slot = lax.broadcasted_iota(jnp.int32, (128, SLOTS), 1)
    spread = jnp.where(slot % (2 * CAP) == lax.broadcasted_iota(jnp.int32, (128, SLOTS), 0), 1.0, 0.0)
    wide = nn(total.astype(BF16), spread.astype(BF16))
    slot = lax.broadcasted_iota(jnp.int32, (SHARDS, SLOTS), 1)
    shard = lax.broadcasted_iota(jnp.int32, (SHARDS, SLOTS), 0)
    shard = shard % X_SIZE * Z_SIZE + shard // X_SIZE
    own = slot // (2 * CAP) == shard
    wide = jnp.sum(jnp.where(own, wide, 0.0), axis=0, keepdims=True)
    rows_ref[...] = wide.astype(jnp.int32) - 1


def relay_kernel(own_ref, *refs):
    got, (keep_ref, give_ref) = refs[:-2], refs[-2:]
    total = got[0][...]
    for one in got[1:]:
        total = total + one[...]
    total = jnp.where(lax.axis_index("section") == 0, own_ref[...], total)
    keep_ref[...] = total[:2 * ROWS]
    give_ref[...] = total[2 * ROWS:]


def send_kernel(slot_ref, keep_ref, got_ref, out_ref):
    own = keep_ref[...] + got_ref[...]
    place = lax.broadcasted_iota(jnp.int32, (SLOTS, ROWS), 0)
    total = None
    for m in range(MICRO):
        cols = slice(m * ROWS, (m + 1) * ROWS)
        hit = (place == slot_ref[0:1, cols]) | (place == slot_ref[1:2, cols])
        part = nt(jnp.where(hit, 1.0, 0.0).astype(BF16), own[cols, :])
        total = part if total is None else total + part
    out_ref[...] = total.astype(BF16)


def owner_kernel(rows_ref, arrived_ref, quot_ref, rem_ref):
    row = lax.broadcasted_iota(jnp.int32, (2 * QROW_DEV, SLOTS), 0)
    picks = jnp.where(row == rows_ref[...], 1.0, 0.0).astype(BF16)
    total = nn(picks, arrived_ref[...])
    quot_ref[...] = total[:QROW_DEV]
    rem_ref[...] = total[QROW_DEV:]


def shards(
    top_grad, layer_inputs, saved_pre, weight_in, weight_out, gain_in, gain_mid, lengths, quot_ids, rem_ids
):
    gain_t, *saved = forward(
        lengths.reshape(MICRO, 4), saved_pre[0], layer_inputs[0], top_grad, gain_mid, gain_in
    )
    *weights, ids = gather_weights(weight_in, weight_out, quot_ids, rem_ids)
    kept = [(*saved[4 * m:4 * m + 3], gain_t) for m in range(MICRO)]
    carried = [saved[4 * m + 3] for m in range(MICRO)]
    before, first = None, None
    for hop in range(SECTIONS):
        section = SECTIONS - 1 - hop
        for micro in range(MICRO):
            last = section == 0 and micro == 1
            extra = () if before is None else (before,)
            if section == 0 and micro == 0:
                extra = extra + (slots, rows)
            out = layer_step(
                section, carried[micro], first if last else None, kept[micro], weights, extra
            )
            if last:
                pieces = out
            elif section == 0:
                before = first = out
            else:
                before = out
                carried[micro] = lax.ppermute(out, "section", [(section, section - 1)])
        if section == 1:
            slots = pl.pallas_call(
                slots_kernel,
                in_specs=[VMEM, VMEM, HBM],
                out_specs=VMEM,
                out_shape=jax.ShapeDtypeStruct((2, MICRO * ROWS), jnp.int32),
                compiler_params=params(16),
                cost_estimate=cost(10**7, 8192),
                name="find_slots",
            )(quot_ids, rem_ids, before)
            rows = pl.pallas_call(
                rows_kernel,
                in_specs=[VMEM, HBM],
                out_specs=VMEM,
                out_shape=jax.ShapeDtypeStruct((1, SLOTS), jnp.int32),
                scratch_shapes=[pltpu.VMEM((SHARDS, 16, ROWS), F32)],
                compiler_params=params(32),
                cost_estimate=cost(3 * 10**7, MIB),
                name="find_rows",
            )(ids, before)

    got = [lax.ppermute(pieces[y], "section", [(0, 2 * y)]) for y in (2, 1, 3)]
    keep, give = pl.pallas_call(
        relay_kernel,
        in_specs=[VMEM] * 4,
        out_specs=[VMEM, VMEM],
        out_shape=[jax.ShapeDtypeStruct((2 * ROWS, ROWS), BF16)] * 2,
        compiler_params=params(16),
        cost_estimate=cost(10**6, MIB),
        name="relay",
    )(pieces[0], *got)
    give = lax.ppermute(give, "section", [(s, s + 1) for s in range(0, SECTIONS, 2)])
    send = pl.pallas_call(
        send_kernel,
        in_specs=[VMEM] * 3,
        out_specs=VMEM,
        out_shape=jax.ShapeDtypeStruct((SLOTS, 128), BF16),
        compiler_params=params(32),
        cost_estimate=cost(7 * 10**7, MIB),
        name="fill_slots",
    )(slots, keep, give)
    arrived = lax.all_to_all(
        send.reshape(SHARDS, 2 * CAP, 128), "shard", split_axis=0, concat_axis=0, tiled=True
    )
    return pl.pallas_call(
        owner_kernel,
        in_specs=[VMEM, VMEM],
        out_specs=[VMEM, VMEM],
        out_shape=[jax.ShapeDtypeStruct((QROW_DEV, 128), F32)] * 2,
        compiler_params=params(32),
        cost_estimate=cost(4 * 10**7, MIB),
        name="owner_sums",
    )(rows, arrived.reshape(SLOTS, 128))


def solution(mesh):
    placed = (
        P(None, "shard", None),
        P("section", None, "shard", None),
        P("section", None, "shard", None),
        P("section", "shard", None),
        P("section", "shard", None),
        P("section", None),
        P("section", None),
        P(None, "shard", None),
        P(None, "shard"),
        P(None, "shard"),
    )
    return jax.shard_map(
        shards,
        mesh=mesh,
        in_specs=placed,
        out_specs=(P("shard", "section"), P("shard", "section")),
        check_vma=False,
    )
```

```python
import functools
import math

import jax
import jax.numpy as jnp
from jax import lax
from jax.experimental import pallas as pl
from jax.experimental.pallas import tpu as pltpu
from jax.sharding import PartitionSpec as P

HEADS = 4
HEAD = 128
ATT = 512
ROWS = 128
WIDTH = 1024
SECTIONS = 8
MICRO = 2
SHARDS = 64
X_SIZE = 4
Z_SIZE = 16
QROW_DEV = 64
CAP = 8
SLOTS = SHARDS * 2 * CAP
EPSILON = 1e-05
BF16 = jnp.bfloat16
F32 = jnp.float32
MIB = 1024 * 1024
VMEM = pl.BlockSpec(memory_space=pltpu.VMEM)
HBM = pl.BlockSpec(memory_space=pl.ANY)

UGR, XHAT, EU, SV, SQ, SK, KT, QT, VN, AN, PT = range(11)
SAVED = 11


def nt(a, b):
    return lax.dot_general(a, b, (((1,), (1,)), ((), ())), preferred_element_type=F32)


def nn(a, b):
    return jnp.dot(a, b, preferred_element_type=F32)


def params(mib):
    return pltpu.CompilerParams(vmem_limit_bytes=mib * MIB)


def cost(flops, size):
    return pl.CostEstimate(flops=flops, bytes_accessed=size, transcendentals=0)


def segment_grid(len_ref, micro, dim):
    place = lax.broadcasted_iota(jnp.int32, (ROWS, ROWS), dim)
    end = jnp.int32(0)
    seg = jnp.zeros((ROWS, ROWS), jnp.int32)
    for k in range(4):
        end = end + len_ref[micro, k]
        seg = seg + (place >= end).astype(jnp.int32)
    return place, seg


def forward_kernel(len_ref, pre_hbm, x_hbm, top_hbm, gain_mid_ref, gain_in_ref, gain_t_ref, *refs):
    out_refs, (pre_ref, x_ref, top_ref, sems) = refs[:4 * MICRO], refs[4 * MICRO:]
    copies = []
    for k, (src, dst) in enumerate(((pre_hbm, pre_ref), (x_hbm, x_ref), (top_hbm, top_ref))):
        for micro in range(MICRO):
            copies.append(pltpu.make_async_copy(src.at[micro], dst.at[micro], sems.at[k, micro]))
            copies[-1].start()
    gain_t_ref[...] = jnp.broadcast_to(gain_in_ref[...], (ROWS, WIDTH)).T
    for one in copies:
        one.wait()
    for micro in range(MICRO):
        saved_ref, xh_ref, rstd_ref, top_t_ref = out_refs[4 * micro:4 * micro + 4]
        forward_part(len_ref, micro, pre_ref, x_ref, top_ref, gain_mid_ref[...],
                     saved_ref, xh_ref, rstd_ref, top_t_ref)


def forward_part(len_ref, micro, pre_ref, x_ref, top_ref, gain, saved_ref, xh_ref, rstd_ref, top_t_ref):
    def act(block):
        pre = pre_ref[micro, :, block * ATT:(block + 1) * ATT].astype(F32)
        sig = jax.nn.sigmoid(pre)
        return pre * sig, sig * (1.0 + pre * (1.0 - sig))

    row, seg_row = segment_grid(len_ref, micro, 0)
    col, seg_col = segment_grid(len_ref, micro, 1)
    same = seg_row == seg_col
    allowed = same & (col <= row)
    allowed_t = same & (row <= col)
    val, dval = act(1)
    que, dque = act(2)
    key, dkey = act(3)
    saved_ref[SV] = dval.T.astype(BF16)
    saved_ref[SQ] = dque.T.astype(BF16)
    saved_ref[SK] = dkey.T.astype(BF16)
    saved_ref[KT] = key.T.astype(BF16)
    saved_ref[QT] = que.T.astype(BF16)
    val, que, key = val.astype(BF16), que.astype(BF16), key.astype(BF16)
    scale = 1.0 / math.sqrt(HEAD)
    mixture = []
    for h in range(HEADS):
        cols = slice(h * HEAD, (h + 1) * HEAD)
        scores = nt(que[:, cols], key[:, cols]) * scale
        soft = jnp.where(allowed, scores * jax.nn.sigmoid(scores), 0.0).astype(BF16)
        scores = nt(key[:, cols], que[:, cols]) * scale
        sig = jax.nn.sigmoid(scores)
        slope = jnp.where(allowed_t, sig * (1.0 + scores * (1.0 - sig)) * scale, 0.0)
        saved_ref[VN, cols, :] = val[:, cols]
        saved_ref[AN, cols, :] = soft
        saved_ref[PT, cols, :] = slope.astype(BF16)
        mixture.append(nn(soft, val[:, cols]))
    mixture = jnp.concatenate(mixture, axis=1)
    centred = mixture - jnp.mean(mixture, axis=1, keepdims=True)
    rstd = lax.rsqrt(jnp.mean(centred * centred, axis=1, keepdims=True) + EPSILON)
    xhat = centred * rstd
    gate, dgate = act(0)
    saved_ref[UGR] = (gate * gain * rstd).T.astype(BF16)
    saved_ref[XHAT] = xhat.T.astype(BF16)
    saved_ref[EU] = (xhat * gain * dgate).T.astype(BF16)
    x = x_ref[micro].astype(F32).T
    x = x - jnp.mean(x, axis=0, keepdims=True)
    rstd = lax.rsqrt(jnp.mean(x * x, axis=0, keepdims=True) + EPSILON)
    xh_ref[...] = (x * rstd).astype(BF16)
    rstd_ref[...] = jnp.broadcast_to(rstd, (8, ROWS))
    top_t_ref[...] = top_ref[micro].astype(F32).T.astype(BF16)


def forward(lengths, pre, x, top, gain_mid, gain_in):
    smem = pl.BlockSpec(memory_space=pltpu.SMEM)
    tall = jax.ShapeDtypeStruct((WIDTH, ROWS), BF16)
    each = [
        jax.ShapeDtypeStruct((SAVED, ATT, ROWS), BF16),
        tall,
        jax.ShapeDtypeStruct((8, ROWS), F32),
        tall,
    ]
    return pl.pallas_call(
        forward_kernel,
        in_specs=[smem] + [pl.BlockSpec(memory_space=pltpu.HBM)] * 3 + [VMEM] * 2,
        out_specs=[VMEM] * 9,
        out_shape=[jax.ShapeDtypeStruct((WIDTH, ROWS), F32)] + each * MICRO,
        scratch_shapes=[
            pltpu.VMEM((MICRO, ROWS, 4 * ATT), BF16),
            pltpu.VMEM((MICRO, ROWS, WIDTH), BF16),
            pltpu.VMEM((MICRO, ROWS, WIDTH), BF16),
            pltpu.SemaphoreType.DMA((3, MICRO)),
        ],
        compiler_params=params(32),
        cost_estimate=cost(2 * 10**8, 6 * MIB),
        name="saved_parts",
    )(lengths, pre, x, top, gain_mid, gain_in)


HALVES = 2048
IDS = HALVES + 512
LINE = IDS + ROWS


def join_kernel(w_in_ref, w_out_ref, quot_ref, rem_ref, out_ref):
    out_ref[:, :HALVES] = w_in_ref[0]
    wide = w_out_ref[0].astype(F32)
    halves = jnp.concatenate([wide[:, :512], wide[:, 512:]], axis=0)
    out_ref[:, HALVES:IDS] = halves.astype(BF16)
    ids = jnp.concatenate([quot_ref[...], rem_ref[...]], axis=0)
    owner = lax.shift_right_logical(ids, 6)
    local = ids - owner * QROW_DEV
    blank = jnp.zeros((8, ROWS), F32)
    coded = jnp.concatenate([owner.astype(F32), local.astype(F32), blank], axis=0)
    out_ref[:, IDS:] = coded.astype(BF16)


def pair_kernel(own_ref, next_ref, out_ref):
    rows = own_ref.shape[0]
    out_ref[:rows, :] = own_ref[...]
    out_ref[rows:, :] = next_ref[...]


def pair(own, other):
    return pl.pallas_call(
        pair_kernel,
        in_specs=[VMEM, VMEM],
        out_specs=VMEM,
        out_shape=jax.ShapeDtypeStruct((2 * own.shape[0], LINE), BF16),
        compiler_params=params(16),
        cost_estimate=cost(1000, 4 * own.shape[0] * LINE * 2),
        name="pair_weights",
    )(own, other)


def along(value, dx, dz):
    pairs = []
    for x in range(X_SIZE):
        for z in range(Z_SIZE):
            to = (x + dx) % X_SIZE * Z_SIZE + (z + dz) % Z_SIZE
            pairs.append((x * Z_SIZE + z, to))
    return lax.ppermute(value, "shard", pairs)


def partner(x, side):
    return (x + 1) % X_SIZE if x % 2 == side else (x - 1) % X_SIZE


def across(value, side):
    pairs = []
    for x in range(X_SIZE):
        pairs += [(x * Z_SIZE + z, partner(x, side) * Z_SIZE + z) for z in range(Z_SIZE)]
    return lax.ppermute(value, "shard", pairs)


def pick_kernel(side, n_blocks, gated, n_after, *refs):
    outs = refs[n_blocks + gated + n_after:]
    if gated:
        outs[1][...] = refs[n_blocks][...]
    here_x = lax.axis_index("shard") // Z_SIZE
    start = pl.multiple_of((here_x + side) % 2 * 16, 16)
    for k, ref in enumerate(refs[:n_blocks]):
        outs[0][k * 16:(k + 1) * 16, :] = ref[pl.ds(start, 16), :]


def pick(side, blocks, gate=None, after=()):
    gates = [] if gate is None else [gate]
    shapes = [jax.ShapeDtypeStruct((16 * len(blocks), LINE), BF16)]
    shapes += [jax.ShapeDtypeStruct((32, LINE), BF16)] * len(gates)
    return pl.pallas_call(
        functools.partial(pick_kernel, side, len(blocks), len(gates), len(after)),
        in_specs=[VMEM] * (len(blocks) + len(gates)) + [HBM] * len(after),
        out_specs=[VMEM] * len(shapes),
        out_shape=shapes,
        compiler_params=params(16),
        cost_estimate=cost(1000, len(blocks) * 160 * 1024),
        name="pick_shards",
    )(*blocks, *gates, *after)


def gather_weights(weight_in, weight_out, quot_ids, rem_ids):
    own = pl.pallas_call(
        join_kernel,
        in_specs=[VMEM] * 4,
        out_specs=VMEM,
        out_shape=jax.ShapeDtypeStruct((16, LINE), BF16),
        compiler_params=params(16),
        cost_estimate=cost(1000, 160 * 1024),
        name="join_weights",
    )(weight_in, weight_out, quot_ids, rem_ids)
    block = pair(own, along(own, -1, 0))
    up, down = {0: block}, {}
    half = Z_SIZE // 2
    blocks, offsets, sizes, sides = [], [], [], ([], [])

    def batch_of(hops):
        batch = []
        for hop in hops:
            batch.append(up[hop])
            offsets.append(-hop)
            if hop in down:
                batch.append(down[hop])
                offsets.append(hop)
        blocks.extend(batch)
        sizes.append(len(batch))
        return batch

    gates = {7: (0, 1, 2, 3, 4, 5)}
    for hop in range(1, half + 1):
        last = down[hop - 1] if hop > 1 else block
        if hop in gates:
            batch = batch_of(gates[hop])
            first, up[hop - 1] = pick(0, batch, up[hop - 1], sides[0][-1:])
            second, last = pick(1, batch, last, sides[1][-1:])
            down[hop - 1] = last
            sides[0].append(across(first, 0))
            sides[1].append(across(second, 1))
        up[hop] = along(up[hop - 1], 0, 1)
        if hop < half:
            down[hop] = along(last, 0, -1)
    batch = batch_of((6, 7, 8))
    for side in range(2):
        sides[side].append(across(pick(side, batch, None, sides[side][-1:])[0], side))
    return pl.pallas_call(
        functools.partial(place_kernel, tuple(offsets), tuple(sizes)),
        in_specs=[VMEM] * (Z_SIZE + 2 * len(sizes)),
        out_specs=[VMEM] * 3,
        out_shape=[
            jax.ShapeDtypeStruct((Z_SIZE, 64, 2048), BF16),
            jax.ShapeDtypeStruct((Z_SIZE, 16, 2048), BF16),
            jax.ShapeDtypeStruct((Z_SIZE, X_SIZE, 16, ROWS), BF16),
        ],
        scratch_shapes=[pltpu.VMEM((Z_SIZE, 32, 1024), F32)],
        compiler_params=params(32),
        cost_estimate=cost(1000, 10 * MIB),
        name="place_weights",
    )(*blocks, *sides[0], *sides[1])


def place_kernel(offsets, sizes, *refs):
    blocks, refs = refs[:Z_SIZE], refs[Z_SIZE:]
    sides = refs[:len(sizes)], refs[len(sizes):2 * len(sizes)]
    w_in_ref, w_out_ref, ids_ref, wide = refs[2 * len(sizes):]
    here_x = lax.axis_index("shard") // Z_SIZE
    here_z = lax.axis_index("shard") % Z_SIZE
    odd = here_x % 2
    spots = [(batch, k) for batch, size in enumerate(sizes) for k in range(size)]
    for block, offset, (batch, k) in zip(blocks, offsets, spots):
        z = (here_z + Z_SIZE + offset) % Z_SIZE
        some = slice(k * 16, (k + 1) * 16)
        sources = (
            (block, slice(0, 16), 0),
            (block, slice(16, 32), 1),
            (sides[0][batch], some, 2 + odd),
            (sides[1][batch], some, 3 - odd),
        )
        for ref, rows, step in sources:
            x = (here_x + step) % X_SIZE
            w_in_ref[z, pl.ds(pl.multiple_of(x * 16, 16), 16), :] = ref[rows, :HALVES]
            ids_ref[z, x] = ref[rows, IDS:]
            halves = ref[rows, HALVES:IDS].astype(F32)
            at = pl.ds(pl.multiple_of(x * 8, 8), 8)
            wide[z, at, 0:512] = halves[0:8]
            wide[z, at, 512:1024] = halves[8:16]
    for z in range(Z_SIZE):
        w_out_ref[z, :, 0:1024] = wide[z, 0:16, :].astype(BF16)
        w_out_ref[z, :, 1024:2048] = wide[z, 16:32, :].astype(BF16)


def step_kernel(at_section, last, n_extra, *refs):
    refs = list(refs)
    g_ref = refs.pop(0)
    first_ref = refs.pop(0) if last else None
    saved, xh, rstd, gain, w_in, w_out = refs[:6]
    outs, gp = refs[6 + n_extra:-1], refs[-1]

    @pl.when(lax.axis_index("section") == at_section)
    def _():
        grad = g_ref[...]
        grad_mid = []
        for half in range(2):
            weight = w_out[:, :, half * 1024:(half + 1) * 1024].reshape(256, 1024)
            both = nn(weight, grad).reshape(Z_SIZE, 2, 8, ROWS)
            grad_mid += [both[:, 0].reshape(HEAD, ROWS), both[:, 1].reshape(HEAD, ROWS)]

        def part(name, h):
            return saved[name, h * HEAD:(h + 1) * HEAD, :]

        terms = [grad_mid[h] * part(UGR, h).astype(F32) for h in range(HEADS)]
        xhats = [part(XHAT, h).astype(F32) for h in range(HEADS)]
        mean_1 = sum(terms[1:], terms[0])
        mean_2 = terms[0] * xhats[0]
        for h in range(1, HEADS):
            mean_2 = mean_2 + terms[h] * xhats[h]
        mean_1 = jnp.sum(mean_1, axis=0, keepdims=True) * (1.0 / ATT)
        mean_2 = jnp.sum(mean_2, axis=0, keepdims=True) * (1.0 / ATT)
        for h in range(HEADS):
            def put(block, value):
                start = block * ATT + h * HEAD
                gp[start:start + HEAD, :] = value.astype(BF16)

            put(0, grad_mid[h] * part(EU, h).astype(F32))
            d_o = (terms[h] - mean_1 - xhats[h] * mean_2).astype(BF16)
            d_s = (nn(part(VN, h), d_o) * part(PT, h).astype(F32)).astype(BF16)
            put(1, nn(d_o, part(AN, h)) * part(SV, h).astype(F32))
            put(2, nn(part(KT, h), d_s) * part(SQ, h).astype(F32))
            put(3, nt(part(QT, h), d_s) * part(SK, h).astype(F32))
        product = nn(w_in[...].reshape(WIDTH, 4 * ATT), gp[...])
        product = product.reshape(Z_SIZE, X_SIZE, 16, ROWS)
        d_xh, x_hat = [], []
        for x in range(X_SIZE):
            rows = slice(x * 256, (x + 1) * 256)
            d_xh.append(product[:, x].reshape(256, ROWS) * gain[rows, :])
            x_hat.append(xh[rows, :].astype(F32))
        mean_1 = sum(d_xh[1:], d_xh[0])
        mean_2 = d_xh[0] * x_hat[0]
        for x in range(1, X_SIZE):
            mean_2 = mean_2 + d_xh[x] * x_hat[x]
        mean_1 = jnp.sum(mean_1, axis=0, keepdims=True) * (1.0 / WIDTH)
        mean_2 = jnp.sum(mean_2, axis=0, keepdims=True) * (1.0 / WIDTH)
        scale = rstd[0:1, :]
        for x in range(X_SIZE):
            rows = slice(x * 256, (x + 1) * 256)
            d_x = (d_xh[x] - mean_1 - x_hat[x] * mean_2) * scale
            result = (grad[rows, :].astype(F32) + d_x).astype(BF16)
            if last:
                outs[x][ROWS:2 * ROWS, :] = result[0:128]
                outs[x][3 * ROWS:, :] = result[128:256]
            else:
                outs[0][rows, :] = result
        if last:
            for x in range(X_SIZE):
                outs[x][0:ROWS, :] = first_ref[x * 256:x * 256 + 128, :]
                outs[x][2 * ROWS:3 * ROWS, :] = first_ref[x * 256 + 128:(x + 1) * 256, :]


def layer_step(at_section, grad, first, kept, weights, extra):
    last = first is not None
    operands = [grad, first] if last else [grad]
    operands += [*kept, *weights]
    if last:
        out_shape = [jax.ShapeDtypeStruct((4 * ROWS, ROWS), BF16)] * (SECTIONS // 2)
    else:
        out_shape = [jax.ShapeDtypeStruct((WIDTH, ROWS), BF16)]
    out = pl.pallas_call(
        functools.partial(step_kernel, at_section, last, len(extra)),
        in_specs=[VMEM] * len(operands) + [HBM] * len(extra),
        out_specs=[VMEM] * len(out_shape),
        out_shape=out_shape,
        scratch_shapes=[pltpu.VMEM((4 * ATT, ROWS), BF16)],
        compiler_params=params(32),
        cost_estimate=cost(7 * 10**8, 8 * MIB),
        name="layer_step",
    )(*operands, *extra)
    return out if last else out[0]


def earlier_mask():
    tokens = MICRO * ROWS
    before = (
        lax.broadcasted_iota(jnp.int32, (tokens, tokens), 0)
        < lax.broadcasted_iota(jnp.int32, (tokens, tokens), 1)
    )
    return jnp.where(before, 1.0, 0.0).astype(BF16)


def slots_kernel(quot_ref, rem_ref, _, slot_ref):
    owners = lax.broadcasted_iota(jnp.int32, (SHARDS, MICRO * ROWS), 0)
    before = earlier_mask()
    for table, ref in enumerate((quot_ref, rem_ref)):
        ids = jnp.concatenate([ref[0:1, :], ref[1:2, :]], axis=1)
        owner = lax.shift_right_logical(ids, 6)
        one_hot = jnp.where(owners == owner, 1.0, 0.0)
        earlier = nn(one_hot.astype(BF16), before)
        rank = jnp.sum(earlier * one_hot, axis=0, keepdims=True).astype(jnp.int32)
        slot_ref[table:table + 1, :] = owner * (2 * CAP) + rank + table * CAP


def rows_kernel(ids_ref, _, rows_ref, wide_ids):
    here = lax.axis_index("shard").astype(F32)
    before = earlier_mask()
    lane = lax.broadcasted_iota(jnp.int32, (SHARDS, 128), 1)
    total = jnp.zeros((SHARDS, 128), F32)
    wide_ids[...] = ids_ref[...].reshape(SHARDS, 16, ROWS).astype(F32)

    def both(row):
        return jnp.concatenate([wide_ids[:, row, :], wide_ids[:, row + 1, :]], axis=1)

    for table in range(2):
        mine = both(2 * table) == here
        rank = nn(jnp.where(mine, 1.0, 0.0).astype(BF16), before)
        local = both(2 * MICRO + 2 * table) + (1.0 + table * QROW_DEV)
        for k in range(CAP):
            value = jnp.where(mine & (rank == float(k)), local, 0.0)
            value = jnp.sum(value, axis=1, keepdims=True)
            total = total + jnp.where(lane == table * CAP + k, value, 0.0)
    slot = lax.broadcasted_iota(jnp.int32, (128, SLOTS), 1)
    spread = jnp.where(slot % (2 * CAP) == lax.broadcasted_iota(jnp.int32, (128, SLOTS), 0), 1.0, 0.0)
    wide = nn(total.astype(BF16), spread.astype(BF16))
    slot = lax.broadcasted_iota(jnp.int32, (SHARDS, SLOTS), 1)
    shard = lax.broadcasted_iota(jnp.int32, (SHARDS, SLOTS), 0)
    shard = shard % X_SIZE * Z_SIZE + shard // X_SIZE
    own = slot // (2 * CAP) == shard
    wide = jnp.sum(jnp.where(own, wide, 0.0), axis=0, keepdims=True)
    rows_ref[...] = wide.astype(jnp.int32) - 1


def relay_kernel(own_ref, *refs):
    got, (keep_ref, give_ref) = refs[:-2], refs[-2:]
    total = got[0][...]
    for one in got[1:]:
        total = total + one[...]
    total = jnp.where(lax.axis_index("section") == 0, own_ref[...], total)
    keep_ref[...] = total[:2 * ROWS]
    give_ref[...] = total[2 * ROWS:]


def send_kernel(slot_ref, keep_ref, got_ref, out_ref):
    own = keep_ref[...] + got_ref[...]
    place = lax.broadcasted_iota(jnp.int32, (SLOTS, ROWS), 0)
    total = None
    for m in range(MICRO):
        cols = slice(m * ROWS, (m + 1) * ROWS)
        hit = (place == slot_ref[0:1, cols]) | (place == slot_ref[1:2, cols])
        part = nt(jnp.where(hit, 1.0, 0.0).astype(BF16), own[cols, :])
        total = part if total is None else total + part
    out_ref[...] = total.astype(BF16)


def owner_kernel(rows_ref, arrived_ref, quot_ref, rem_ref):
    row = lax.broadcasted_iota(jnp.int32, (2 * QROW_DEV, SLOTS), 0)
    picks = jnp.where(row == rows_ref[...], 1.0, 0.0).astype(BF16)
    total = nn(picks, arrived_ref[...])
    quot_ref[...] = total[:QROW_DEV]
    rem_ref[...] = total[QROW_DEV:]


def shards(
    top_grad, layer_inputs, saved_pre, weight_in, weight_out, gain_in, gain_mid, lengths, quot_ids, rem_ids
):
    gain_t, *saved = forward(
        lengths.reshape(MICRO, 4), saved_pre[0], layer_inputs[0], top_grad, gain_mid, gain_in
    )
    *weights, ids = gather_weights(weight_in, weight_out, quot_ids, rem_ids)
    kept = [(*saved[4 * m:4 * m + 3], gain_t) for m in range(MICRO)]
    carried = [saved[4 * m + 3] for m in range(MICRO)]
    before, first = None, None
    for hop in range(SECTIONS):
        section = SECTIONS - 1 - hop
        for micro in range(MICRO):
            last = section == 0 and micro == 1
            extra = () if before is None else (before,)
            if section == 0 and micro == 0:
                extra = extra + (slots, rows)
            out = layer_step(
                section, carried[micro], first if last else None, kept[micro], weights, extra
            )
            if last:
                pieces = out
            elif section == 0:
                before = first = out
            else:
                before = out
                carried[micro] = lax.ppermute(out, "section", [(section, section - 1)])
        if section == 1:
            slots = pl.pallas_call(
                slots_kernel,
                in_specs=[VMEM, VMEM, HBM],
                out_specs=VMEM,
                out_shape=jax.ShapeDtypeStruct((2, MICRO * ROWS), jnp.int32),
                compiler_params=params(16),
                cost_estimate=cost(10**7, 8192),
                name="find_slots",
            )(quot_ids, rem_ids, before)
            rows = pl.pallas_call(
                rows_kernel,
                in_specs=[VMEM, HBM],
                out_specs=VMEM,
                out_shape=jax.ShapeDtypeStruct((1, SLOTS), jnp.int32),
                scratch_shapes=[pltpu.VMEM((SHARDS, 16, ROWS), F32)],
                compiler_params=params(32),
                cost_estimate=cost(3 * 10**7, MIB),
                name="find_rows",
            )(ids, before)

    got = [lax.ppermute(pieces[y], "section", [(0, 2 * y)]) for y in (2, 1, 3)]
    keep, give = pl.pallas_call(
        relay_kernel,
        in_specs=[VMEM] * 4,
        out_specs=[VMEM, VMEM],
        out_shape=[jax.ShapeDtypeStruct((2 * ROWS, ROWS), BF16)] * 2,
        compiler_params=params(16),
        cost_estimate=cost(10**6, MIB),
        name="relay",
    )(pieces[0], *got)
    give = lax.ppermute(give, "section", [(s, s + 1) for s in range(0, SECTIONS, 2)])
    send = pl.pallas_call(
        send_kernel,
        in_specs=[VMEM] * 3,
        out_specs=VMEM,
        out_shape=jax.ShapeDtypeStruct((SLOTS, 128), BF16),
        compiler_params=params(32),
        cost_estimate=cost(7 * 10**7, MIB),
        name="fill_slots",
    )(slots, keep, give)
    arrived = lax.all_to_all(
        send.reshape(SHARDS, 2 * CAP, 128), "shard", split_axis=0, concat_axis=0, tiled=True
    )
    return pl.pallas_call(
        owner_kernel,
        in_specs=[VMEM, VMEM],
        out_specs=[VMEM, VMEM],
        out_shape=[jax.ShapeDtypeStruct((QROW_DEV, 128), F32)] * 2,
        compiler_params=params(32),
        cost_estimate=cost(4 * 10**7, MIB),
        name="owner_sums",
    )(rows, arrived.reshape(SLOTS, 128))


def solution(mesh):
    placed = (
        P(None, "shard", None),
        P("section", None, "shard", None),
        P("section", None, "shard", None),
        P("section", "shard", None),
        P("section", "shard", None),
        P("section", None),
        P("section", None),
        P(None, "shard", None),
        P(None, "shard"),
        P(None, "shard"),
    )
    return jax.shard_map(
        shards,
        mesh=mesh,
        in_specs=placed,
        out_specs=(P("shard", "section"), P("shard", "section")),
        check_vma=False,
    )
```

```python
import functools
import math

import jax
import jax.numpy as jnp
from jax import lax
from jax.experimental import pallas as pl
from jax.experimental.pallas import tpu as pltpu
from jax.sharding import PartitionSpec as P

HEADS = 4
HEAD = 128
ATT = 512
ROWS = 128
WIDTH = 1024
SECTIONS = 8
MICRO = 2
SHARDS = 64
X_SIZE = 4
Z_SIZE = 16
QROW_DEV = 64
CAP = 8
SLOTS = SHARDS * 2 * CAP
EPSILON = 1e-05
BF16 = jnp.bfloat16
F32 = jnp.float32
MIB = 1024 * 1024
VMEM = pl.BlockSpec(memory_space=pltpu.VMEM)
HBM = pl.BlockSpec(memory_space=pl.ANY)

UGR, XHAT, EU, SV, SQ, SK, KT, QT, VN, AN, PT = range(11)
SAVED = 11


def nt(a, b):
    return lax.dot_general(a, b, (((1,), (1,)), ((), ())), preferred_element_type=F32)


def nn(a, b):
    return jnp.dot(a, b, preferred_element_type=F32)


def params(mib):
    return pltpu.CompilerParams(vmem_limit_bytes=mib * MIB)


def cost(flops, size):
    return pl.CostEstimate(flops=flops, bytes_accessed=size, transcendentals=0)


def segment_grid(len_ref, micro, dim):
    place = lax.broadcasted_iota(jnp.int32, (ROWS, ROWS), dim)
    end = jnp.int32(0)
    seg = jnp.zeros((ROWS, ROWS), jnp.int32)
    for k in range(4):
        end = end + len_ref[micro, k]
        seg = seg + (place >= end).astype(jnp.int32)
    return place, seg


def forward_kernel(len_ref, pre_hbm, x_hbm, top_hbm, gain_mid_ref, gain_in_ref, gain_t_ref, *refs):
    out_refs, (pre_ref, x_ref, top_ref, sems) = refs[:4 * MICRO], refs[4 * MICRO:]
    copies = []
    for k, (src, dst) in enumerate(((pre_hbm, pre_ref), (x_hbm, x_ref), (top_hbm, top_ref))):
        for micro in range(MICRO):
            copies.append(pltpu.make_async_copy(src.at[micro], dst.at[micro], sems.at[k, micro]))
            copies[-1].start()
    gain_t_ref[...] = jnp.broadcast_to(gain_in_ref[...], (ROWS, WIDTH)).T
    for one in copies:
        one.wait()
    for micro in range(MICRO):
        saved_ref, xh_ref, rstd_ref, top_t_ref = out_refs[4 * micro:4 * micro + 4]
        forward_part(len_ref, micro, pre_ref, x_ref, top_ref, gain_mid_ref[...],
                     saved_ref, xh_ref, rstd_ref, top_t_ref)


def forward_part(len_ref, micro, pre_ref, x_ref, top_ref, gain, saved_ref, xh_ref, rstd_ref, top_t_ref):
    def act(block):
        pre = pre_ref[micro, :, block * ATT:(block + 1) * ATT].astype(F32)
        sig = jax.nn.sigmoid(pre)
        return pre * sig, sig * (1.0 + pre * (1.0 - sig))

    row, seg_row = segment_grid(len_ref, micro, 0)
    col, seg_col = segment_grid(len_ref, micro, 1)
    same = seg_row == seg_col
    allowed = same & (col <= row)
    allowed_t = same & (row <= col)
    val, dval = act(1)
    que, dque = act(2)
    key, dkey = act(3)
    saved_ref[SV] = dval.T.astype(BF16)
    saved_ref[SQ] = dque.T.astype(BF16)
    saved_ref[SK] = dkey.T.astype(BF16)
    saved_ref[KT] = key.T.astype(BF16)
    saved_ref[QT] = que.T.astype(BF16)
    val, que, key = val.astype(BF16), que.astype(BF16), key.astype(BF16)
    scale = 1.0 / math.sqrt(HEAD)
    mixture = []
    for h in range(HEADS):
        cols = slice(h * HEAD, (h + 1) * HEAD)
        scores = nt(que[:, cols], key[:, cols]) * scale
        soft = jnp.where(allowed, scores * jax.nn.sigmoid(scores), 0.0).astype(BF16)
        scores = nt(key[:, cols], que[:, cols]) * scale
        sig = jax.nn.sigmoid(scores)
        slope = jnp.where(allowed_t, sig * (1.0 + scores * (1.0 - sig)) * scale, 0.0)
        saved_ref[VN, cols, :] = val[:, cols]
        saved_ref[AN, cols, :] = soft
        saved_ref[PT, cols, :] = slope.astype(BF16)
        mixture.append(nn(soft, val[:, cols]))
    mixture = jnp.concatenate(mixture, axis=1)
    centred = mixture - jnp.mean(mixture, axis=1, keepdims=True)
    rstd = lax.rsqrt(jnp.mean(centred * centred, axis=1, keepdims=True) + EPSILON)
    xhat = centred * rstd
    gate, dgate = act(0)
    saved_ref[UGR] = (gate * gain * rstd).T.astype(BF16)
    saved_ref[XHAT] = xhat.T.astype(BF16)
    saved_ref[EU] = (xhat * gain * dgate).T.astype(BF16)
    x = x_ref[micro].astype(F32).T
    x = x - jnp.mean(x, axis=0, keepdims=True)
    rstd = lax.rsqrt(jnp.mean(x * x, axis=0, keepdims=True) + EPSILON)
    xh_ref[...] = (x * rstd).astype(BF16)
    rstd_ref[...] = jnp.broadcast_to(rstd, (8, ROWS))
    top_t_ref[...] = top_ref[micro].astype(F32).T.astype(BF16)


def forward(lengths, pre, x, top, gain_mid, gain_in):
    smem = pl.BlockSpec(memory_space=pltpu.SMEM)
    tall = jax.ShapeDtypeStruct((WIDTH, ROWS), BF16)
    each = [
        jax.ShapeDtypeStruct((SAVED, ATT, ROWS), BF16),
        tall,
        jax.ShapeDtypeStruct((8, ROWS), F32),
        tall,
    ]
    return pl.pallas_call(
        forward_kernel,
        in_specs=[smem] + [pl.BlockSpec(memory_space=pltpu.HBM)] * 3 + [VMEM] * 2,
        out_specs=[VMEM] * 9,
        out_shape=[jax.ShapeDtypeStruct((WIDTH, ROWS), F32)] + each * MICRO,
        scratch_shapes=[
            pltpu.VMEM((MICRO, ROWS, 4 * ATT), BF16),
            pltpu.VMEM((MICRO, ROWS, WIDTH), BF16),
            pltpu.VMEM((MICRO, ROWS, WIDTH), BF16),
            pltpu.SemaphoreType.DMA((3, MICRO)),
        ],
        compiler_params=params(32),
        cost_estimate=cost(2 * 10**8, 6 * MIB),
        name="saved_parts",
    )(lengths, pre, x, top, gain_mid, gain_in)


HALVES = 2048
IDS = HALVES + 512
LINE = IDS + ROWS


def join_kernel(w_in_ref, w_out_ref, quot_ref, rem_ref, out_ref):
    out_ref[:, :HALVES] = w_in_ref[0]
    wide = w_out_ref[0].astype(F32)
    halves = jnp.concatenate([wide[:, :512], wide[:, 512:]], axis=0)
    out_ref[:, HALVES:IDS] = halves.astype(BF16)
    ids = jnp.concatenate([quot_ref[...], rem_ref[...]], axis=0)
    owner = lax.shift_right_logical(ids, 6)
    local = ids - owner * QROW_DEV
    blank = jnp.zeros((8, ROWS), F32)
    coded = jnp.concatenate([owner.astype(F32), local.astype(F32), blank], axis=0)
    out_ref[:, IDS:] = coded.astype(BF16)


def pair_kernel(own_ref, next_ref, out_ref):
    rows = own_ref.shape[0]
    out_ref[:rows, :] = own_ref[...]
    out_ref[rows:, :] = next_ref[...]


def pair(own, other):
    return pl.pallas_call(
        pair_kernel,
        in_specs=[VMEM, VMEM],
        out_specs=VMEM,
        out_shape=jax.ShapeDtypeStruct((2 * own.shape[0], LINE), BF16),
        compiler_params=params(16),
        cost_estimate=cost(1000, 4 * own.shape[0] * LINE * 2),
        name="pair_weights",
    )(own, other)


def along(value, dx, dz):
    pairs = []
    for x in range(X_SIZE):
        for z in range(Z_SIZE):
            to = (x + dx) % X_SIZE * Z_SIZE + (z + dz) % Z_SIZE
            pairs.append((x * Z_SIZE + z, to))
    return lax.ppermute(value, "shard", pairs)


def partner(x, side):
    return (x + 1) % X_SIZE if x % 2 == side else (x - 1) % X_SIZE


def across(value, side):
    pairs = []
    for x in range(X_SIZE):
        pairs += [(x * Z_SIZE + z, partner(x, side) * Z_SIZE + z) for z in range(Z_SIZE)]
    return lax.ppermute(value, "shard", pairs)


def pick_kernel(side, n_blocks, gated, n_after, *refs):
    outs = refs[n_blocks + gated + n_after:]
    if gated:
        outs[1][...] = refs[n_blocks][...]
    here_x = lax.axis_index("shard") // Z_SIZE
    start = pl.multiple_of((here_x + side) % 2 * 16, 16)
    for k, ref in enumerate(refs[:n_blocks]):
        outs[0][k * 16:(k + 1) * 16, :] = ref[pl.ds(start, 16), :]


def pick(side, blocks, gate=None, after=()):
    gates = [] if gate is None else [gate]
    shapes = [jax.ShapeDtypeStruct((16 * len(blocks), LINE), BF16)]
    shapes += [jax.ShapeDtypeStruct((32, LINE), BF16)] * len(gates)
    return pl.pallas_call(
        functools.partial(pick_kernel, side, len(blocks), len(gates), len(after)),
        in_specs=[VMEM] * (len(blocks) + len(gates)) + [HBM] * len(after),
        out_specs=[VMEM] * len(shapes),
        out_shape=shapes,
        compiler_params=params(16),
        cost_estimate=cost(1000, len(blocks) * 160 * 1024),
        name="pick_shards",
    )(*blocks, *gates, *after)


def gather_weights(weight_in, weight_out, quot_ids, rem_ids):
    own = pl.pallas_call(
        join_kernel,
        in_specs=[VMEM] * 4,
        out_specs=VMEM,
        out_shape=jax.ShapeDtypeStruct((16, LINE), BF16),
        compiler_params=params(16),
        cost_estimate=cost(1000, 160 * 1024),
        name="join_weights",
    )(weight_in, weight_out, quot_ids, rem_ids)
    block = pair(own, along(own, -1, 0))
    up, down = {0: block}, {}
    half = Z_SIZE // 2
    blocks, offsets, sizes, sides = [], [], [], ([], [])

    def batch_of(hops):
        batch = []
        for hop in hops:
            batch.append(up[hop])
            offsets.append(-hop)
            if hop in down:
                batch.append(down[hop])
                offsets.append(hop)
        blocks.extend(batch)
        sizes.append(len(batch))
        return batch

    gates = {6: (0, 1, 2, 3, 4)}
    for hop in range(1, half + 1):
        last = down[hop - 1] if hop > 1 else block
        if hop in gates:
            batch = batch_of(gates[hop])
            first, up[hop - 1] = pick(0, batch, up[hop - 1], sides[0][-1:])
            second, last = pick(1, batch, last, sides[1][-1:])
            down[hop - 1] = last
            sides[0].append(across(first, 0))
            sides[1].append(across(second, 1))
        up[hop] = along(up[hop - 1], 0, 1)
        if hop < half:
            down[hop] = along(last, 0, -1)
    batch = batch_of((5, 6, 7, 8))
    for side in range(2):
        sides[side].append(across(pick(side, batch, None, sides[side][-1:])[0], side))
    return pl.pallas_call(
        functools.partial(place_kernel, tuple(offsets), tuple(sizes)),
        in_specs=[VMEM] * (Z_SIZE + 2 * len(sizes)),
        out_specs=[VMEM] * 3,
        out_shape=[
            jax.ShapeDtypeStruct((Z_SIZE, 64, 2048), BF16),
            jax.ShapeDtypeStruct((Z_SIZE, 16, 2048), BF16),
            jax.ShapeDtypeStruct((Z_SIZE, X_SIZE, 16, ROWS), BF16),
        ],
        scratch_shapes=[pltpu.VMEM((Z_SIZE, 32, 1024), F32)],
        compiler_params=params(32),
        cost_estimate=cost(1000, 10 * MIB),
        name="place_weights",
    )(*blocks, *sides[0], *sides[1])


def place_kernel(offsets, sizes, *refs):
    blocks, refs = refs[:Z_SIZE], refs[Z_SIZE:]
    sides = refs[:len(sizes)], refs[len(sizes):2 * len(sizes)]
    w_in_ref, w_out_ref, ids_ref, wide = refs[2 * len(sizes):]
    here_x = lax.axis_index("shard") // Z_SIZE
    here_z = lax.axis_index("shard") % Z_SIZE
    odd = here_x % 2
    spots = [(batch, k) for batch, size in enumerate(sizes) for k in range(size)]
    for block, offset, (batch, k) in zip(blocks, offsets, spots):
        z = (here_z + Z_SIZE + offset) % Z_SIZE
        some = slice(k * 16, (k + 1) * 16)
        sources = (
            (block, slice(0, 16), 0),
            (block, slice(16, 32), 1),
            (sides[0][batch], some, 2 + odd),
            (sides[1][batch], some, 3 - odd),
        )
        for ref, rows, step in sources:
            x = (here_x + step) % X_SIZE
            w_in_ref[z, pl.ds(pl.multiple_of(x * 16, 16), 16), :] = ref[rows, :HALVES]
            ids_ref[z, x] = ref[rows, IDS:]
            halves = ref[rows, HALVES:IDS].astype(F32)
            at = pl.ds(pl.multiple_of(x * 8, 8), 8)
            wide[z, at, 0:512] = halves[0:8]
            wide[z, at, 512:1024] = halves[8:16]
    for z in range(Z_SIZE):
        w_out_ref[z, :, 0:1024] = wide[z, 0:16, :].astype(BF16)
        w_out_ref[z, :, 1024:2048] = wide[z, 16:32, :].astype(BF16)


def step_kernel(at_section, last, n_extra, *refs):
    refs = list(refs)
    g_ref = refs.pop(0)
    first_ref = refs.pop(0) if last else None
    saved, xh, rstd, gain, w_in, w_out = refs[:6]
    outs, gp = refs[6 + n_extra:-1], refs[-1]

    @pl.when(lax.axis_index("section") == at_section)
    def _():
        grad = g_ref[...]
        grad_mid = []
        for half in range(2):
            weight = w_out[:, :, half * 1024:(half + 1) * 1024].reshape(256, 1024)
            both = nn(weight, grad).reshape(Z_SIZE, 2, 8, ROWS)
            grad_mid += [both[:, 0].reshape(HEAD, ROWS), both[:, 1].reshape(HEAD, ROWS)]

        def part(name, h):
            return saved[name, h * HEAD:(h + 1) * HEAD, :]

        terms = [grad_mid[h] * part(UGR, h).astype(F32) for h in range(HEADS)]
        xhats = [part(XHAT, h).astype(F32) for h in range(HEADS)]
        mean_1 = sum(terms[1:], terms[0])
        mean_2 = terms[0] * xhats[0]
        for h in range(1, HEADS):
            mean_2 = mean_2 + terms[h] * xhats[h]
        mean_1 = jnp.sum(mean_1, axis=0, keepdims=True) * (1.0 / ATT)
        mean_2 = jnp.sum(mean_2, axis=0, keepdims=True) * (1.0 / ATT)
        for h in range(HEADS):
            def put(block, value):
                start = block * ATT + h * HEAD
                gp[start:start + HEAD, :] = value.astype(BF16)

            put(0, grad_mid[h] * part(EU, h).astype(F32))
            d_o = (terms[h] - mean_1 - xhats[h] * mean_2).astype(BF16)
            d_s = (nn(part(VN, h), d_o) * part(PT, h).astype(F32)).astype(BF16)
            put(1, nn(d_o, part(AN, h)) * part(SV, h).astype(F32))
            put(2, nn(part(KT, h), d_s) * part(SQ, h).astype(F32))
            put(3, nt(part(QT, h), d_s) * part(SK, h).astype(F32))
        product = nn(w_in[...].reshape(WIDTH, 4 * ATT), gp[...])
        product = product.reshape(Z_SIZE, X_SIZE, 16, ROWS)
        d_xh, x_hat = [], []
        for x in range(X_SIZE):
            rows = slice(x * 256, (x + 1) * 256)
            d_xh.append(product[:, x].reshape(256, ROWS) * gain[rows, :])
            x_hat.append(xh[rows, :].astype(F32))
        mean_1 = sum(d_xh[1:], d_xh[0])
        mean_2 = d_xh[0] * x_hat[0]
        for x in range(1, X_SIZE):
            mean_2 = mean_2 + d_xh[x] * x_hat[x]
        mean_1 = jnp.sum(mean_1, axis=0, keepdims=True) * (1.0 / WIDTH)
        mean_2 = jnp.sum(mean_2, axis=0, keepdims=True) * (1.0 / WIDTH)
        scale = rstd[0:1, :]
        for x in range(X_SIZE):
            rows = slice(x * 256, (x + 1) * 256)
            d_x = (d_xh[x] - mean_1 - x_hat[x] * mean_2) * scale
            result = (grad[rows, :].astype(F32) + d_x).astype(BF16)
            if last:
                outs[x][ROWS:2 * ROWS, :] = result[0:128]
                outs[x][3 * ROWS:, :] = result[128:256]
            else:
                outs[0][rows, :] = result
        if last:
            for x in range(X_SIZE):
                outs[x][0:ROWS, :] = first_ref[x * 256:x * 256 + 128, :]
                outs[x][2 * ROWS:3 * ROWS, :] = first_ref[x * 256 + 128:(x + 1) * 256, :]


def layer_step(at_section, grad, first, kept, weights, extra):
    last = first is not None
    operands = [grad, first] if last else [grad]
    operands += [*kept, *weights]
    if last:
        out_shape = [jax.ShapeDtypeStruct((4 * ROWS, ROWS), BF16)] * (SECTIONS // 2)
    else:
        out_shape = [jax.ShapeDtypeStruct((WIDTH, ROWS), BF16)]
    out = pl.pallas_call(
        functools.partial(step_kernel, at_section, last, len(extra)),
        in_specs=[VMEM] * len(operands) + [HBM] * len(extra),
        out_specs=[VMEM] * len(out_shape),
        out_shape=out_shape,
        scratch_shapes=[pltpu.VMEM((4 * ATT, ROWS), BF16)],
        compiler_params=params(32),
        cost_estimate=cost(7 * 10**8, 8 * MIB),
        name="layer_step",
    )(*operands, *extra)
    return out if last else out[0]


def earlier_mask():
    tokens = MICRO * ROWS
    before = (
        lax.broadcasted_iota(jnp.int32, (tokens, tokens), 0)
        < lax.broadcasted_iota(jnp.int32, (tokens, tokens), 1)
    )
    return jnp.where(before, 1.0, 0.0).astype(BF16)


def slots_kernel(quot_ref, rem_ref, _, slot_ref):
    owners = lax.broadcasted_iota(jnp.int32, (SHARDS, MICRO * ROWS), 0)
    before = earlier_mask()
    for table, ref in enumerate((quot_ref, rem_ref)):
        ids = jnp.concatenate([ref[0:1, :], ref[1:2, :]], axis=1)
        owner = lax.shift_right_logical(ids, 6)
        one_hot = jnp.where(owners == owner, 1.0, 0.0)
        earlier = nn(one_hot.astype(BF16), before)
        rank = jnp.sum(earlier * one_hot, axis=0, keepdims=True).astype(jnp.int32)
        slot_ref[table:table + 1, :] = owner * (2 * CAP) + rank + table * CAP


def rows_kernel(ids_ref, _, rows_ref, wide_ids):
    here = lax.axis_index("shard").astype(F32)
    before = earlier_mask()
    lane = lax.broadcasted_iota(jnp.int32, (SHARDS, 128), 1)
    total = jnp.zeros((SHARDS, 128), F32)
    wide_ids[...] = ids_ref[...].reshape(SHARDS, 16, ROWS).astype(F32)

    def both(row):
        return jnp.concatenate([wide_ids[:, row, :], wide_ids[:, row + 1, :]], axis=1)

    for table in range(2):
        mine = both(2 * table) == here
        rank = nn(jnp.where(mine, 1.0, 0.0).astype(BF16), before)
        local = both(2 * MICRO + 2 * table) + (1.0 + table * QROW_DEV)
        for k in range(CAP):
            value = jnp.where(mine & (rank == float(k)), local, 0.0)
            value = jnp.sum(value, axis=1, keepdims=True)
            total = total + jnp.where(lane == table * CAP + k, value, 0.0)
    slot = lax.broadcasted_iota(jnp.int32, (128, SLOTS), 1)
    spread = jnp.where(slot % (2 * CAP) == lax.broadcasted_iota(jnp.int32, (128, SLOTS), 0), 1.0, 0.0)
    wide = nn(total.astype(BF16), spread.astype(BF16))
    slot = lax.broadcasted_iota(jnp.int32, (SHARDS, SLOTS), 1)
    shard = lax.broadcasted_iota(jnp.int32, (SHARDS, SLOTS), 0)
    shard = shard % X_SIZE * Z_SIZE + shard // X_SIZE
    own = slot // (2 * CAP) == shard
    wide = jnp.sum(jnp.where(own, wide, 0.0), axis=0, keepdims=True)
    rows_ref[...] = wide.astype(jnp.int32) - 1


def relay_kernel(own_ref, *refs):
    got, (keep_ref, give_ref) = refs[:-2], refs[-2:]
    total = got[0][...]
    for one in got[1:]:
        total = total + one[...]
    total = jnp.where(lax.axis_index("section") == 0, own_ref[...], total)
    keep_ref[...] = total[:2 * ROWS]
    give_ref[...] = total[2 * ROWS:]


def send_kernel(slot_ref, keep_ref, got_ref, out_ref):
    own = keep_ref[...] + got_ref[...]
    place = lax.broadcasted_iota(jnp.int32, (SLOTS, ROWS), 0)
    total = None
    for m in range(MICRO):
        cols = slice(m * ROWS, (m + 1) * ROWS)
        hit = (place == slot_ref[0:1, cols]) | (place == slot_ref[1:2, cols])
        part = nt(jnp.where(hit, 1.0, 0.0).astype(BF16), own[cols, :])
        total = part if total is None else total + part
    out_ref[...] = total.astype(BF16)


def owner_kernel(rows_ref, arrived_ref, quot_ref, rem_ref):
    row = lax.broadcasted_iota(jnp.int32, (2 * QROW_DEV, SLOTS), 0)
    picks = jnp.where(row == rows_ref[...], 1.0, 0.0).astype(BF16)
    total = nn(picks, arrived_ref[...])
    quot_ref[...] = total[:QROW_DEV]
    rem_ref[...] = total[QROW_DEV:]


def shards(
    top_grad, layer_inputs, saved_pre, weight_in, weight_out, gain_in, gain_mid, lengths, quot_ids, rem_ids
):
    gain_t, *saved = forward(
        lengths.reshape(MICRO, 4), saved_pre[0], layer_inputs[0], top_grad, gain_mid, gain_in
    )
    *weights, ids = gather_weights(weight_in, weight_out, quot_ids, rem_ids)
    kept = [(*saved[4 * m:4 * m + 3], gain_t) for m in range(MICRO)]
    carried = [saved[4 * m + 3] for m in range(MICRO)]
    before, first = None, None
    for hop in range(SECTIONS):
        section = SECTIONS - 1 - hop
        for micro in range(MICRO):
            last = section == 0 and micro == 1
            extra = () if before is None else (before,)
            if section == 0 and micro == 0:
                extra = extra + (slots, rows)
            out = layer_step(
                section, carried[micro], first if last else None, kept[micro], weights, extra
            )
            if last:
                pieces = out
            elif section == 0:
                before = first = out
            else:
                before = out
                carried[micro] = lax.ppermute(out, "section", [(section, section - 1)])
        if section == 1:
            slots = pl.pallas_call(
                slots_kernel,
                in_specs=[VMEM, VMEM, HBM],
                out_specs=VMEM,
                out_shape=jax.ShapeDtypeStruct((2, MICRO * ROWS), jnp.int32),
                compiler_params=params(16),
                cost_estimate=cost(10**7, 8192),
                name="find_slots",
            )(quot_ids, rem_ids, before)
            rows = pl.pallas_call(
                rows_kernel,
                in_specs=[VMEM, HBM],
                out_specs=VMEM,
                out_shape=jax.ShapeDtypeStruct((1, SLOTS), jnp.int32),
                scratch_shapes=[pltpu.VMEM((SHARDS, 16, ROWS), F32)],
                compiler_params=params(32),
                cost_estimate=cost(3 * 10**7, MIB),
                name="find_rows",
            )(ids, before)

    got = [lax.ppermute(pieces[y], "section", [(0, 2 * y)]) for y in (2, 1, 3)]
    keep, give = pl.pallas_call(
        relay_kernel,
        in_specs=[VMEM] * 4,
        out_specs=[VMEM, VMEM],
        out_shape=[jax.ShapeDtypeStruct((2 * ROWS, ROWS), BF16)] * 2,
        compiler_params=params(16),
        cost_estimate=cost(10**6, MIB),
        name="relay",
    )(pieces[0], *got)
    give = lax.ppermute(give, "section", [(s, s + 1) for s in range(0, SECTIONS, 2)])
    send = pl.pallas_call(
        send_kernel,
        in_specs=[VMEM] * 3,
        out_specs=VMEM,
        out_shape=jax.ShapeDtypeStruct((SLOTS, 128), BF16),
        compiler_params=params(32),
        cost_estimate=cost(7 * 10**7, MIB),
        name="fill_slots",
    )(slots, keep, give)
    arrived = lax.all_to_all(
        send.reshape(SHARDS, 2 * CAP, 128), "shard", split_axis=0, concat_axis=0, tiled=True
    )
    return pl.pallas_call(
        owner_kernel,
        in_specs=[VMEM, VMEM],
        out_specs=[VMEM, VMEM],
        out_shape=[jax.ShapeDtypeStruct((QROW_DEV, 128), F32)] * 2,
        compiler_params=params(32),
        cost_estimate=cost(4 * 10**7, MIB),
        name="owner_sums",
    )(rows, arrived.reshape(SLOTS, 128))


def solution(mesh):
    placed = (
        P(None, "shard", None),
        P("section", None, "shard", None),
        P("section", None, "shard", None),
        P("section", "shard", None),
        P("section", "shard", None),
        P("section", None),
        P("section", None),
        P(None, "shard", None),
        P(None, "shard"),
        P(None, "shard"),
    )
    return jax.shard_map(
        shards,
        mesh=mesh,
        in_specs=placed,
        out_specs=(P("shard", "section"), P("shard", "section")),
        check_vma=False,
    )
```
